32 devices in a mesh: freq: 2 (over core), depth: 16 (over z, y, x).
Axes of the slice: x: 2, y: 2, z: 4, core: 2. Of those that a mesh axis runs over, the one named last changes fastest.
Arguments:
- green_source: bfloat16 [4, 16, 384, 2, 256], P('freq', 'depth'), may hold values from -6 to 6
- green_receiver: bfloat16 [4, 16, 128, 2, 256], P('freq', 'depth'), may hold values from -6 to 6
- source_index: int32 [1024], replicated, may hold values from 0 to 383
- receiver_index: int32 [1024], replicated, may hold values from 0 to 127
- frequency_bins: int32 [4], P('freq'), may hold values from 0 to 127
- depth_profile: float32 [16], P('depth'), may hold values from 0.5 to 2
Outputs:
- kernels: float32 [4, 1024, 16], P(None, ('freq', 'depth'))
The draws below stay inside these ranges and needn't reach their ends.
All inputs are finite; a program needn't handle non-finite values.
Results may differ from the reference program's by a relative error of at most 0.0015.
Values may be sent and summed in bfloat16 or wider, within the bound.
No kernel may reach another device: no remote copies, remote signals or barrier semaphores. Data moves between devices by JAX's collectives and lax.ppermute only.
A program may use at most 64 MiB of HBM per device.

```python
import math
import jax
import jax.numpy as jnp
from jax import lax

NBINS = 128
W = 4
Z = 16
HS = 384
HR = 128
WX = 16
WY = 16
NP = 1024


def place_ends(drawn, own_key, smallest, high):
    longest = drawn.shape.index(max(drawn.shape))
    spots = []
    for shift in (0, 1):
        where = [jax.random.randint(jax.random.fold_in(own_key, axis), (), 0, length) for axis, length in enumerate(drawn.shape)]
        where[longest] = (where[longest] + shift) % drawn.shape[longest]
        spots.append(tuple(where))
    return drawn.at[spots[0]].set(smallest).at[spots[1]].set(high)


def block_levels(rng, dims, split, least, top_value):
    factor_of = 1.0
    for axis_at, shards_of in split:
        heights = jax.random.uniform(jax.random.fold_in(jax.random.fold_in(rng, 6), axis_at), (shards_of,), jnp.float32, least / len(split), top_value / len(split))
        factor_of = factor_of * jnp.repeat(jnp.exp(heights), dims[axis_at] // shards_of).reshape((-1,) + (1,) * (len(dims) - 1 - axis_at))
    return factor_of


def normal_values(stream_key, shape, deviation, limit, pieces=(), held_as=jnp.bfloat16):
    values = jax.random.normal(stream_key, shape, jnp.float32) * deviation
    if len(pieces) > 0:
        values = block_levels(stream_key, shape, pieces, -0.22, 0.18) * values
    return jnp.clip(values, min=-limit, max=limit).astype(held_as)


def setup_inputs(seed: int = 0) -> dict:
    streams_of = jax.random.split(jax.random.key(seed), 7)
    green_source = normal_values(streams_of[0], (W, Z, HS, 2, WX * WY), 1.0, 6.0, ((0, 2), (1, 16)))
    green_receiver = normal_values(streams_of[1], (W, Z, HR, 2, WX * WY), 1.0, 6.0, ((0, 2), (1, 16)))
    source_index = place_ends(jax.random.randint(streams_of[2], (NP,), 0, HS), jax.random.fold_in(streams_of[2], 1), 0, HS - 1).astype(jnp.int32)
    receiver_index = place_ends(jax.random.randint(streams_of[3], (NP,), 0, HR), jax.random.fold_in(streams_of[3], 1), 0, HR - 1).astype(jnp.int32)
    frequency_bins = place_ends(jax.random.randint(streams_of[4], (W,), 0, NBINS), jax.random.fold_in(streams_of[4], 1), 0, NBINS - 1).astype(jnp.int32)
    depth_profile = jnp.clip(jnp.exp(math.log(2.0) - 1.3862944 * jax.random.uniform(streams_of[5], (Z,), jnp.float32) ** block_levels(streams_of[5], (Z,), ((0, 16),), -0.2, 0.2)), 0.5, 2.0)
    return {"green_source": green_source, "green_receiver": green_receiver, "source_index": source_index, "receiver_index": receiver_index, "frequency_bins": frequency_bins, "depth_profile": depth_profile}


def window_slope(values, direction):
    window = values.reshape(values.shape[:-1] + (WX, WY))
    axis_index = window.ndim - 2 + direction
    extent = window.shape[axis_index]
    widths = [(0, 0)] * axis_index + [(1, 1)] + [(0, 0)] * (window.ndim - axis_index - 1)
    padded = jnp.pad(window, widths)
    upper = lax.slice_in_dim(padded, 2, extent + 2, axis=axis_index)
    lower = lax.slice_in_dim(padded, 0, extent, axis=axis_index)
    return (0.5 * (upper - lower)).reshape(values.shape)

def source_rows(current, layer_above, layer_below):
    real_part = current[..., 0, :]
    imag_part = current[..., 1, :]
    real_wide = real_part.astype(jnp.float32)
    imag_wide = imag_part.astype(jnp.float32)
    slope_real_x = window_slope(real_wide, 0).astype(jnp.bfloat16)
    slope_imag_x = window_slope(imag_wide, 0).astype(jnp.bfloat16)
    slope_real_y = window_slope(real_wide, 1).astype(jnp.bfloat16)
    slope_imag_y = window_slope(imag_wide, 1).astype(jnp.bfloat16)
    blocks = [jnp.concatenate([real_part, -imag_part], axis=-1), jnp.concatenate([slope_imag_x, slope_real_x], axis=-1), jnp.concatenate([slope_imag_y, slope_real_y], axis=-1), jnp.concatenate([layer_above[..., 1, :], layer_above[..., 0, :]], axis=-1), jnp.concatenate([layer_below[..., 1, :], layer_below[..., 0, :]], axis=-1)]
    return jnp.stack(blocks, axis=-3)

def reference(green_source, green_receiver, source_index, receiver_index, frequency_bins, depth_profile):
    scaled_freq = 0.5 + frequency_bins.astype(jnp.float32) / NBINS
    kernel_scale = 1.0 / math.sqrt(2.0 * WX * WY * W)

    def depth_layer(level):
        current = lax.dynamic_index_in_dim(green_source, level, axis=1, keepdims=False)
        upper_level = jnp.minimum(level + 1, Z - 1).astype(jnp.int32)
        lower_level = jnp.maximum(level - 1, 0).astype(jnp.int32)
        layer_above = lax.dynamic_index_in_dim(green_source, upper_level, axis=1, keepdims=False)
        layer_below = lax.dynamic_index_in_dim(green_source, lower_level, axis=1, keepdims=False)
        layer_above = jnp.where(level + 1 < Z, layer_above, jnp.zeros_like(layer_above))
        layer_below = jnp.where(level >= 1, layer_below, jnp.zeros_like(layer_below))
        left_rows = source_rows(current, layer_above, layer_below)
        left_pairs = left_rows[:, :, source_index].astype(jnp.float32)
        receiver_rows = lax.dynamic_index_in_dim(green_receiver, level, axis=1, keepdims=False)
        receiver_rows = receiver_rows.reshape(W, HR, 2 * WX * WY)
        right_pairs = receiver_rows[:, receiver_index].astype(jnp.float32)
        picked = jnp.einsum('wkpm,wpm->wkp', left_pairs, right_pairs)
        coupling = lax.dynamic_index_in_dim(depth_profile, level, axis=0, keepdims=False)
        first = picked[:, 0] * (scaled_freq * scaled_freq)[:, None] * coupling
        second = picked[:, 1] * scaled_freq[:, None]
        third = picked[:, 2] * scaled_freq[:, None]
        fourth = 0.5 * (picked[:, 3] - picked[:, 4]) * scaled_freq[:, None]
        stacked = jnp.stack([first, second, third, fourth], axis=1)
        return lax.optimization_barrier(jnp.sum(stacked, axis=0)) * kernel_scale
    layers = lax.map(depth_layer, jnp.arange(Z, dtype=jnp.int32))
    return jnp.transpose(layers, (1, 2, 0))
```

```python
import functools
import math

import jax
import jax.numpy as jnp
from jax import lax
from jax.experimental import pallas as pl
from jax.experimental.pallas import tpu as pltpu
from jax.sharding import PartitionSpec as P

NBINS = 128
WX = 16
WY = 16
LANES = 128
ROWS = 8
VMEM_BYTES = 48 * 1024 * 1024

TRANSPOSED = (((1,), (1,)), ((), ()))


def dot(left, right):
    return jnp.dot(left, right, preferred_element_type=jnp.float32)


def dot_t(left, right):
    return lax.dot_general(left, right, TRANSPOSED, preferred_element_type=jnp.float32)


def frequency_weight(bins_ref, slot):
    return 0.5 + bins_ref[slot].astype(jnp.float32) / NBINS


def slope_table(cells):
    source = lax.broadcasted_iota(jnp.int32, (cells, cells), 0)
    target = lax.broadcasted_iota(jnp.int32, (cells, cells), 1)
    column = lax.rem(target, WY)
    step = source - target
    half, zero = jnp.float32(0.5), jnp.float32(0.0)
    along_x = jnp.where(step == WY, half, zero) - jnp.where(step == -WY, half, zero)
    along_y = jnp.where((step == 1) & (column != WY - 1), half, zero) - jnp.where(
        (step == -1) & (column != 0), half, zero
    )
    return jnp.concatenate([along_x, along_y], axis=1).astype(jnp.bfloat16)


def pick_pairs(products, source_ref, receiver_ref, count, receivers):
    sources = products.shape[1]
    pairs = source_ref.shape[1]
    at_source = lax.broadcasted_iota(jnp.int32, (sources, pairs), 0) == source_ref[...]
    hot = jnp.where(at_source, jnp.float32(1), jnp.float32(0)).astype(jnp.bfloat16)
    high = products.astype(jnp.bfloat16)
    low = (products - high.astype(jnp.float32)).astype(jnp.bfloat16)
    picked = dot(high, hot) + dot(low, hot)
    at_receiver = lax.broadcasted_iota(jnp.int32, (receivers, pairs), 0) == receiver_ref[...]
    return [
        jnp.sum(
            jnp.where(at_receiver, picked[k * receivers : (k + 1) * receivers], 0.0),
            axis=0,
            keepdims=True,
        )
        for k in range(count)
    ]


def local_terms(
    scale, bins_ref, profile_ref, source_ref, receiver_ref, green_s, green_r, out_ref
):
    freqs, _, _, cells = green_s.shape
    receivers = green_r.shape[2]
    table = slope_table(cells)
    sound = along_x = along_y = 0.0
    for slot in range(freqs):
        weight = frequency_weight(bins_ref, slot)
        real, imag = green_s[slot, 0], green_s[slot, 1]
        slope_real = dot(real, table).astype(jnp.bfloat16)
        slope_imag = dot(imag, table).astype(jnp.bfloat16)
        near_real, near_imag = green_r[slot, 0], green_r[slot, 1]
        plain = dot_t(near_real, real) - dot_t(near_imag, imag)
        slope_x = dot_t(near_imag, slope_real[:, :cells]) + dot_t(near_real, slope_imag[:, :cells])
        slope_y = dot_t(near_imag, slope_real[:, cells:]) + dot_t(near_real, slope_imag[:, cells:])
        sound = sound + plain * (weight * weight * profile_ref[0] * scale)
        along_x = along_x + slope_x * (weight * scale)
        along_y = along_y + slope_y * (weight * scale)
    products = jnp.concatenate([sound, along_x, along_y], axis=0)
    rows = pick_pairs(products, source_ref, receiver_ref, 3, receivers)
    blank = jnp.zeros((ROWS - 3, rows[0].shape[1]), jnp.float32)
    out_ref[...] = jnp.concatenate(rows + [blank], axis=0)


def layer_terms(
    scale, share, bins_ref, source_ref, receiver_ref, green_s, lower_r, upper_r, terms, out_ref
):
    freqs = green_s.shape[0]
    receivers = lower_r.shape[2]
    total = 0.0
    for slot in range(freqs):
        weight = frequency_weight(bins_ref, slot)
        near_real = jnp.concatenate([lower_r[slot, 0], upper_r[slot, 0]], axis=0)
        near_imag = jnp.concatenate([lower_r[slot, 1], upper_r[slot, 1]], axis=0)
        both = dot_t(near_imag, green_s[slot, 0]) + dot_t(near_real, green_s[slot, 1])
        total = total + both * (0.5 * weight * scale)
    rows = pick_pairs(total, source_ref, receiver_ref, 2, receivers)
    blank = jnp.zeros((ROWS - 5, rows[0].shape[1]), jnp.float32)
    block = jnp.concatenate([terms[0:3, :]] + rows + [blank], axis=0)
    for owner in range(out_ref.shape[0]):
        tile = owner * share // LANES
        out_ref[owner] = block[:, tile * LANES : (tile + 1) * LANES]


def combine(freqs, depths, share, parts_ref, out_ref):
    owner = lax.axis_index("freq") * depths + lax.axis_index("depth")
    offset = lax.rem(owner * share, LANES)

    def term(k):
        total = parts_ref[pl.ds(0, depths), k, :]
        for group in range(1, freqs):
            total = total + parts_ref[pl.ds(group * depths, depths), k, :]
        return total

    blank = jnp.zeros((1, LANES), jnp.float32)
    from_above = jnp.concatenate([term(3)[1:], blank], axis=0)
    from_below = jnp.concatenate([blank, term(4)[:-1]], axis=0)
    for k, value in enumerate([term(0), term(1), term(2), from_above - from_below]):
        out_ref[k] = pltpu.roll(value, lax.rem(LANES - offset, LANES), 1)[:, :share]


def vmem(count):
    return [pl.BlockSpec(memory_space=pltpu.VMEM)] * count


def smem(count):
    return [pl.BlockSpec(memory_space=pltpu.SMEM)] * count


def on_device(
    green_source, green_receiver, source_index, receiver_index, frequency_bins, depth_profile
):
    local_freqs, _, sources, _, cells = green_source.shape
    receivers = green_receiver.shape[2]
    pairs = source_index.shape[0]
    n_freq, n_depth = lax.axis_size("freq"), lax.axis_size("depth")
    owners = n_freq * n_depth
    share = pairs // owners
    scale = 1.0 / math.sqrt(2.0 * WX * WY * local_freqs * n_freq)
    params = pltpu.CompilerParams(vmem_limit_bytes=VMEM_BYTES)

    near = jnp.swapaxes(green_receiver[:, 0], 1, 2)
    forward = [(i, i + 1) for i in range(n_depth - 1)]
    backward = [(target, source) for source, target in forward]
    lower = lax.ppermute(near, "depth", forward)
    upper = lax.ppermute(near, "depth", backward)

    far = jnp.swapaxes(green_source[:, 0], 1, 2)
    source_row = source_index.reshape(1, pairs)
    receiver_row = receiver_index.reshape(1, pairs)
    product = 2 * 2 * cells * local_freqs * sources * receivers
    picking = 2 * 2 * sources * receivers * pairs
    terms = pl.pallas_call(
        functools.partial(local_terms, scale),
        out_shape=jax.ShapeDtypeStruct((ROWS, pairs), jnp.float32),
        in_specs=smem(2) + vmem(4),
        out_specs=pl.BlockSpec(memory_space=pltpu.VMEM),
        compiler_params=params,
        cost_estimate=pl.CostEstimate(
            flops=3 * (product + picking), bytes_accessed=1 << 21, transcendentals=0
        ),
        name="local_terms",
    )(frequency_bins, depth_profile, source_row, receiver_row, far, near)
    parts = pl.pallas_call(
        functools.partial(layer_terms, scale, share),
        out_shape=jax.ShapeDtypeStruct((owners, ROWS, LANES), jnp.float32),
        in_specs=smem(1) + vmem(6),
        out_specs=pl.BlockSpec(memory_space=pltpu.VMEM),
        compiler_params=params,
        cost_estimate=pl.CostEstimate(
            flops=2 * (product + picking), bytes_accessed=1 << 21, transcendentals=0
        ),
        name="layer_terms",
    )(frequency_bins, source_row, receiver_row, far, lower, upper, terms)
    parts = lax.all_to_all(parts, ("freq", "depth"), split_axis=0, concat_axis=0, tiled=True)
    kernels = pl.pallas_call(
        functools.partial(combine, n_freq, n_depth, share),
        out_shape=jax.ShapeDtypeStruct((4, n_depth, share), jnp.float32),
        in_specs=vmem(1),
        out_specs=pl.BlockSpec(memory_space=pltpu.VMEM),
        compiler_params=params,
        name="combine",
    )(parts)
    return jnp.swapaxes(kernels, 1, 2)


def solution(mesh):
    placed = (
        P("freq", "depth", None, None, None),
        P("freq", "depth", None, None, None),
        P(),
        P(),
        P("freq"),
        P("depth"),
    )
    return jax.shard_map(
        on_device,
        mesh=mesh,
        in_specs=placed,
        out_specs=P(None, ("freq", "depth"), None),
        check_vma=False,
    )
```

```python
import functools
import math

import jax
import jax.numpy as jnp
from jax import lax
from jax.experimental import pallas as pl
from jax.experimental.pallas import tpu as pltpu
from jax.sharding import PartitionSpec as P

NBINS = 128
WX = 16
WY = 16
LANES = 128
VMEM_BYTES = 48 * 1024 * 1024


def dot(left, right):
    return jnp.dot(left, right, preferred_element_type=jnp.float32)


def frequency_weight(bins_ref, slot):
    return 0.5 + bins_ref[slot].astype(jnp.float32) / NBINS


def slope_table(cells):
    target = lax.broadcasted_iota(jnp.int32, (cells, cells), 0)
    source = lax.broadcasted_iota(jnp.int32, (cells, cells), 1)
    column = lax.rem(target, WY)
    step = source - target
    half, zero = jnp.float32(0.5), jnp.float32(0.0)
    along_x = jnp.where(step == WY, half, zero) - jnp.where(step == -WY, half, zero)
    along_y = jnp.where((step == 1) & (column != WY - 1), half, zero) - jnp.where(
        (step == -1) & (column != 0), half, zero
    )
    return jnp.concatenate([along_x, along_y], axis=0).astype(jnp.bfloat16)


def pick_pairs(products, hot, receiver_ref):
    receivers = products.shape[0]
    pairs = receiver_ref.shape[1]
    high = products.astype(jnp.bfloat16)
    low = (products - high.astype(jnp.float32)).astype(jnp.bfloat16)
    both = dot(jnp.concatenate([high, low], axis=0), hot)
    picked = both[:receivers] + both[receivers:]
    at_receiver = lax.broadcasted_iota(jnp.int32, (receivers, pairs), 0) == receiver_ref[...]
    row = jnp.sum(jnp.where(at_receiver, picked, 0.0), axis=0, keepdims=True)
    return jnp.concatenate(
        [row[:, at : at + LANES] for at in range(0, pairs, LANES)], axis=0
    )


def local_terms(
    scale, bins_ref, profile_ref, source_ref, receiver_ref, green_s, green_r, out_ref, hot_ref
):
    freqs, _, cells, sources = green_s.shape
    pairs = source_ref.shape[1]
    at_source = lax.broadcasted_iota(jnp.int32, (sources, pairs), 0) == source_ref[...]
    hot_ref[...] = jnp.where(at_source, jnp.float32(1), jnp.float32(0)).astype(jnp.bfloat16)
    table = slope_table(cells)
    sound = along_x = along_y = 0.0
    for slot in range(freqs):
        weight = frequency_weight(bins_ref, slot)
        real, imag = green_s[slot, 0], green_s[slot, 1]
        slope_real = dot(table, real).astype(jnp.bfloat16)
        slope_imag = dot(table, imag).astype(jnp.bfloat16)
        near_real, near_imag = green_r[slot, 0], green_r[slot, 1]
        plain = dot(near_real, real) - dot(near_imag, imag)
        slope_x = dot(near_imag, slope_real[:cells]) + dot(near_real, slope_imag[:cells])
        slope_y = dot(near_imag, slope_real[cells:]) + dot(near_real, slope_imag[cells:])
        sound = sound + plain * (weight * weight * profile_ref[0] * scale)
        along_x = along_x + slope_x * (weight * scale)
        along_y = along_y + slope_y * (weight * scale)
    hot = hot_ref[...]
    for k, products in enumerate([sound, along_x, along_y]):
        out_ref[k] = pick_pairs(products, hot, receiver_ref)


def layer_term(scale, bins_ref, receiver_ref, hot, green_s, other_r):
    total = 0.0
    for slot in range(green_s.shape[0]):
        both = dot(other_r[slot, 1], green_s[slot, 0]) + dot(other_r[slot, 0], green_s[slot, 1])
        total = total + both * (0.5 * frequency_weight(bins_ref, slot) * scale)
    return pick_pairs(total, hot, receiver_ref)


def near_term(scale, bins_ref, receiver_ref, hot_ref, green_s, near_r, out_ref):
    out_ref[...] = layer_term(scale, bins_ref, receiver_ref, hot_ref[...], green_s, near_r)


def far_term(
    scale, share, bins_ref, receiver_ref, hot_ref, green_s, far_r, terms, near_ref, out_ref
):
    far = layer_term(scale, bins_ref, receiver_ref, hot_ref[...], green_s, far_r)
    near = near_ref[...]
    odd = lax.rem(lax.axis_index("depth"), 2) == 1
    below = jnp.where(odd, near, far)
    above = jnp.where(odd, far, near)
    tiles = far.shape[0]
    group = lax.broadcasted_iota(jnp.int32, (tiles, LANES), 1) // share
    in_tile = LANES // share

    def moved(value, to, part):
        return pltpu.roll(value, (to - part) * share % LANES, 1) if to != part else value

    for part in range(in_tile):
        first = moved(below, 3, part)
        for k in range(3):
            first = jnp.where(group == k, moved(terms[k], k, part), first)
        out_ref[pl.ds(2 * part, tiles, stride=2 * in_tile), :] = first
        out_ref[pl.ds(2 * part + 1, tiles, stride=2 * in_tile), :] = moved(above, 0, part)


def combine(freqs, depths, share, parts_ref, out_ref):
    def row(which):
        total = parts_ref[pl.ds(which, depths, stride=2), :]
        for group in range(1, freqs):
            total = total + parts_ref[pl.ds(2 * group * depths + which, depths, stride=2), :]
        return total

    first = row(0)
    above = row(1)[:, :share]
    for k in range(3):
        out_ref[k] = first[:, k * share : (k + 1) * share]
    below = first[:, 3 * share : 4 * share]
    blank = jnp.zeros((1, share), jnp.float32)
    out_ref[3] = jnp.concatenate([below[1:], blank], axis=0) - jnp.concatenate(
        [blank, above[:-1]], axis=0
    )


def vmem(count):
    return [pl.BlockSpec(memory_space=pltpu.VMEM)] * count


def smem(count):
    return [pl.BlockSpec(memory_space=pltpu.SMEM)] * count


def on_device(
    green_source, green_receiver, source_index, receiver_index, frequency_bins, depth_profile
):
    local_freqs, _, sources, _, cells = green_source.shape
    receivers = green_receiver.shape[2]
    pairs = source_index.shape[0]
    n_freq, n_depth = lax.axis_size("freq"), lax.axis_size("depth")
    owners = n_freq * n_depth
    share = pairs // owners
    tiles = pairs // LANES
    scale = 1.0 / math.sqrt(2.0 * WX * WY * local_freqs * n_freq)
    params = pltpu.CompilerParams(vmem_limit_bytes=VMEM_BYTES)

    own = jnp.swapaxes(green_receiver[:, 0], 1, 2)
    paired = [(i, i ^ 1) for i in range(n_depth)]
    crossed = [(i, i + 1) for i in range(1, n_depth - 1, 2)]
    crossed += [(target, source) for source, target in crossed]
    near_r = lax.ppermute(own, "depth", paired)
    far_r = lax.ppermute(own, "depth", crossed)

    green_s = jnp.transpose(green_source[:, 0], (0, 2, 3, 1))
    source_row = source_index.reshape(1, pairs)
    receiver_row = receiver_index.reshape(1, pairs)
    product = 2 * 2 * cells * local_freqs * sources * receivers
    picking = 2 * 2 * sources * receivers * pairs

    def call(body, name, shapes, n_smem, n_vmem, terms):
        return pl.pallas_call(
            body,
            out_shape=shapes,
            in_specs=smem(n_smem) + vmem(n_vmem),
            out_specs=jax.tree.map(lambda _: pl.BlockSpec(memory_space=pltpu.VMEM), shapes),
            compiler_params=params,
            cost_estimate=pl.CostEstimate(
                flops=terms * (product + picking), bytes_accessed=1 << 21, transcendentals=0
            ),
            name=name,
        )

    term_shape = jax.ShapeDtypeStruct((tiles, LANES), jnp.float32)
    terms, hot = call(
        functools.partial(local_terms, scale),
        "local_terms",
        [
            jax.ShapeDtypeStruct((3, tiles, LANES), jnp.float32),
            jax.ShapeDtypeStruct((sources, pairs), jnp.bfloat16),
        ],
        2, 4, 3,
    )(frequency_bins, depth_profile, source_row, receiver_row, green_s, own)
    near = call(functools.partial(near_term, scale), "near_term", term_shape, 1, 4, 1)(
        frequency_bins, receiver_row, hot, green_s, near_r
    )
    parts = call(
        functools.partial(far_term, scale, share),
        "far_term",
        jax.ShapeDtypeStruct((2 * owners, LANES), jnp.float32),
        1, 6, 1,
    )(frequency_bins, receiver_row, hot, green_s, far_r, terms, near)
    parts = lax.all_to_all(parts, ("freq", "depth"), split_axis=0, concat_axis=0, tiled=True)
    kernels = call(
        functools.partial(combine, n_freq, n_depth, share),
        "combine",
        jax.ShapeDtypeStruct((4, n_depth, share), jnp.float32),
        0, 1, 0,
    )(parts)
    return jnp.swapaxes(kernels, 1, 2)


def solution(mesh):
    placed = (
        P("freq", "depth", None, None, None),
        P("freq", "depth", None, None, None),
        P(),
        P(),
        P("freq"),
        P("depth"),
    )
    return jax.shard_map(
        on_device,
        mesh=mesh,
        in_specs=placed,
        out_specs=P(None, ("freq", "depth"), None),
        check_vma=False,
    )
```

```python
import functools
import math

import jax
import jax.numpy as jnp
from jax import lax
from jax.experimental import pallas as pl
from jax.experimental.pallas import tpu as pltpu
from jax.sharding import PartitionSpec as P

NBINS = 128
WX = 16
WY = 16
LANES = 128
VMEM_BYTES = 48 * 1024 * 1024


def dot(left, right):
    return jnp.dot(left, right, preferred_element_type=jnp.float32)


def frequency_weight(bins_ref, slot):
    return 0.5 + bins_ref[slot].astype(jnp.float32) / NBINS


def slope_table(cells):
    target = lax.broadcasted_iota(jnp.int32, (cells, cells), 0)
    source = lax.broadcasted_iota(jnp.int32, (cells, cells), 1)
    column = lax.rem(target, WY)
    step = source - target
    half, zero = jnp.float32(0.5), jnp.float32(0.0)
    along_x = jnp.where(step == WY, half, zero) - jnp.where(step == -WY, half, zero)
    along_y = jnp.where((step == 1) & (column != WY - 1), half, zero) - jnp.where(
        (step == -1) & (column != 0), half, zero
    )
    return jnp.concatenate([along_x, along_y], axis=0).astype(jnp.bfloat16)


def pick_pairs(products, hot, receiver_ref):
    receivers = products.shape[0]
    pairs = receiver_ref.shape[1]
    high = products.astype(jnp.bfloat16)
    low = (products - high.astype(jnp.float32)).astype(jnp.bfloat16)
    both = dot(jnp.concatenate([high, low], axis=0), hot)
    picked = both[:receivers] + both[receivers:]
    at_receiver = lax.broadcasted_iota(jnp.int32, (receivers, pairs), 0) == receiver_ref[...]
    row = jnp.sum(jnp.where(at_receiver, picked, 0.0), axis=0, keepdims=True)
    return jnp.concatenate(
        [row[:, at : at + LANES] for at in range(0, pairs, LANES)], axis=0
    )


def local_terms(
    scale,
    bins_ref,
    profile_ref,
    source_ref,
    receiver_ref,
    green_s,
    green_r,
    out_ref,
    hot_ref,
    weight_ref,
):
    freqs, _, cells, sources = green_s.shape
    pairs = source_ref.shape[1]
    at_source = lax.broadcasted_iota(jnp.int32, (sources, pairs), 0) == source_ref[...]
    hot_ref[...] = jnp.where(at_source, jnp.float32(1), jnp.float32(0)).astype(jnp.bfloat16)
    table = slope_table(cells)
    sound = along_x = along_y = 0.0
    for slot in range(freqs):
        weight = frequency_weight(bins_ref, slot)
        weight_ref[slot] = jnp.full(weight_ref.shape[1:], 0.5 * weight * scale, jnp.float32)
        real, imag = green_s[slot, 0], green_s[slot, 1]
        slope_real = dot(table, real).astype(jnp.bfloat16)
        slope_imag = dot(table, imag).astype(jnp.bfloat16)
        near_real, near_imag = green_r[slot, 0], green_r[slot, 1]
        plain = dot(near_real, real) - dot(near_imag, imag)
        slope_x = dot(near_imag, slope_real[:cells]) + dot(near_real, slope_imag[:cells])
        slope_y = dot(near_imag, slope_real[cells:]) + dot(near_real, slope_imag[cells:])
        sound = sound + plain * (weight * weight * profile_ref[0] * scale)
        along_x = along_x + slope_x * (weight * scale)
        along_y = along_y + slope_y * (weight * scale)
    hot = hot_ref[...]
    for k, products in enumerate([sound, along_x, along_y]):
        out_ref[k] = pick_pairs(products, hot, receiver_ref)


def layer_term(weight_ref, receiver_ref, hot, green_s, other_r):
    total = 0.0
    for slot in range(green_s.shape[0]):
        both = dot(other_r[slot, 1], green_s[slot, 0]) + dot(other_r[slot, 0], green_s[slot, 1])
        total = total + both * weight_ref[slot]
    return pick_pairs(total, hot, receiver_ref)


def near_term(weight_ref, receiver_ref, hot_ref, green_s, near_r, out_ref):
    out_ref[...] = layer_term(weight_ref, receiver_ref, hot_ref[...], green_s, near_r)


def far_term(
    share, weight_ref, receiver_ref, hot_ref, green_s, far_r, terms, near_ref, out_ref
):
    far = layer_term(weight_ref, receiver_ref, hot_ref[...], green_s, far_r)
    near = near_ref[...]
    odd = lax.rem(lax.axis_index("depth"), 2) == 1
    below = jnp.where(odd, near, far)
    above = jnp.where(odd, far, near)
    tiles = far.shape[0]
    group = lax.broadcasted_iota(jnp.int32, (tiles, LANES), 1) // share
    in_tile = LANES // share

    def moved(value, to, part):
        return pltpu.roll(value, (to - part) * share % LANES, 1) if to != part else value

    for part in range(in_tile):
        first = moved(below, 3, part)
        for k in range(3):
            first = jnp.where(group == k, moved(terms[k], k, part), first)
        out_ref[pl.ds(2 * part, tiles, stride=2 * in_tile), :] = first
        out_ref[pl.ds(2 * part + 1, tiles, stride=2 * in_tile), :] = moved(above, 0, part)


def combine(freqs, depths, share, parts_ref, out_ref):
    def row(which):
        total = parts_ref[pl.ds(which, depths, stride=2), :]
        for group in range(1, freqs):
            total = total + parts_ref[pl.ds(2 * group * depths + which, depths, stride=2), :]
        return total

    first = row(0)
    above = row(1)[:, :share]
    for k in range(3):
        out_ref[k] = first[:, k * share : (k + 1) * share]
    below = first[:, 3 * share : 4 * share]
    blank = jnp.zeros((1, share), jnp.float32)
    out_ref[3] = jnp.concatenate([below[1:], blank], axis=0) - jnp.concatenate(
        [blank, above[:-1]], axis=0
    )


def vmem(count):
    return [pl.BlockSpec(memory_space=pltpu.VMEM)] * count


def smem(count):
    return [pl.BlockSpec(memory_space=pltpu.SMEM)] * count


def on_device(
    green_source, green_receiver, source_index, receiver_index, frequency_bins, depth_profile
):
    local_freqs, _, sources, _, cells = green_source.shape
    receivers = green_receiver.shape[2]
    pairs = source_index.shape[0]
    n_freq, n_depth = lax.axis_size("freq"), lax.axis_size("depth")
    owners = n_freq * n_depth
    share = pairs // owners
    tiles = pairs // LANES
    scale = 1.0 / math.sqrt(2.0 * WX * WY * local_freqs * n_freq)
    params = pltpu.CompilerParams(vmem_limit_bytes=VMEM_BYTES)

    own = jnp.swapaxes(green_receiver[:, 0], 1, 2)
    paired = [(i, i ^ 1) for i in range(n_depth)]
    crossed = [(i, i + 1) for i in range(1, n_depth - 1, 2)]
    crossed += [(target, source) for source, target in crossed]
    near_r = lax.ppermute(own, "depth", paired)
    far_r = lax.ppermute(own, "depth", crossed)

    green_s = jnp.transpose(green_source[:, 0], (0, 2, 3, 1))
    source_row = source_index.reshape(1, pairs)
    receiver_row = receiver_index.reshape(1, pairs)
    product = 2 * 2 * cells * local_freqs * sources * receivers
    picking = 2 * 2 * sources * receivers * pairs

    def call(body, name, shapes, n_smem, n_vmem, terms):
        return pl.pallas_call(
            body,
            out_shape=shapes,
            in_specs=smem(n_smem) + vmem(n_vmem),
            out_specs=jax.tree.map(lambda _: pl.BlockSpec(memory_space=pltpu.VMEM), shapes),
            compiler_params=params,
            cost_estimate=pl.CostEstimate(
                flops=terms * (product + picking), bytes_accessed=1 << 21, transcendentals=0
            ),
            name=name,
        )

    term_shape = jax.ShapeDtypeStruct((tiles, LANES), jnp.float32)
    terms, hot, weights = call(
        functools.partial(local_terms, scale),
        "local_terms",
        [
            jax.ShapeDtypeStruct((3, tiles, LANES), jnp.float32),
            jax.ShapeDtypeStruct((sources, pairs), jnp.bfloat16),
            jax.ShapeDtypeStruct((local_freqs, 1, sources), jnp.float32),
        ],
        2, 4, 3,
    )(frequency_bins, depth_profile, source_row, receiver_row, green_s, own)
    near = call(near_term, "near_term", term_shape, 0, 5, 1)(
        weights, receiver_row, hot, green_s, near_r
    )
    parts = call(
        functools.partial(far_term, share),
        "far_term",
        jax.ShapeDtypeStruct((2 * owners, LANES), jnp.float32),
        0, 7, 1,
    )(weights, receiver_row, hot, green_s, far_r, terms, near)
    parts = lax.all_to_all(parts, ("freq", "depth"), split_axis=0, concat_axis=0, tiled=True)
    kernels = call(
        functools.partial(combine, n_freq, n_depth, share),
        "combine",
        jax.ShapeDtypeStruct((4, n_depth, share), jnp.float32),
        0, 1, 0,
    )(parts)
    return jnp.swapaxes(kernels, 1, 2)


def solution(mesh):
    placed = (
        P("freq", "depth", None, None, None),
        P("freq", "depth", None, None, None),
        P(),
        P(),
        P("freq"),
        P("depth"),
    )
    return jax.shard_map(
        on_device,
        mesh=mesh,
        in_specs=placed,
        out_specs=P(None, ("freq", "depth"), None),
        check_vma=False,
    )
```

```python
import functools
import math

import jax
import jax.numpy as jnp
from jax import lax
from jax.experimental import pallas as pl
from jax.experimental.pallas import tpu as pltpu
from jax.sharding import PartitionSpec as P

NBINS = 128
WX = 16
WY = 16
LANES = 128
VMEM_BYTES = 48 * 1024 * 1024


def dot(left, right):
    return jnp.dot(left, right, preferred_element_type=jnp.float32)


def frequency_weight(bins_ref, slot):
    return 0.5 + bins_ref[slot].astype(jnp.float32) / NBINS


def slope_table(cells):
    target = lax.broadcasted_iota(jnp.int32, (cells, cells), 0)
    source = lax.broadcasted_iota(jnp.int32, (cells, cells), 1)
    column = lax.rem(target, WY)
    step = source - target
    half, zero = jnp.float32(0.5), jnp.float32(0.0)
    along_x = jnp.where(step == WY, half, zero) - jnp.where(step == -WY, half, zero)
    along_y = jnp.where((step == 1) & (column != WY - 1), half, zero) - jnp.where(
        (step == -1) & (column != 0), half, zero
    )
    return jnp.concatenate([along_x, along_y], axis=0).astype(jnp.bfloat16)


def pick_pairs(products, hot, receiver_ref):
    receivers = products.shape[0]
    pairs = receiver_ref.shape[1]
    high = products.astype(jnp.bfloat16)
    low = (products - high.astype(jnp.float32)).astype(jnp.bfloat16)
    both = dot(jnp.concatenate([high, low], axis=0), hot)
    picked = both[:receivers] + both[receivers:]
    at_receiver = lax.broadcasted_iota(jnp.int32, (receivers, pairs), 0) == receiver_ref[...]
    row = jnp.sum(jnp.where(at_receiver, picked, 0.0), axis=0, keepdims=True)
    return jnp.concatenate(
        [row[:, at : at + LANES] for at in range(0, pairs, LANES)], axis=0
    )


def local_terms(
    scale,
    bins_ref,
    profile_ref,
    source_ref,
    receiver_ref,
    green_s,
    green_r,
    out_ref,
    hot_ref,
    weight_ref,
):
    freqs, _, cells, sources = green_s.shape
    pairs = source_ref.shape[1]
    at_source = lax.broadcasted_iota(jnp.int32, (sources, pairs), 0) == source_ref[...]
    hot_ref[...] = jnp.where(at_source, jnp.float32(1), jnp.float32(0)).astype(jnp.bfloat16)
    table = slope_table(cells)
    sound = along_x = along_y = 0.0
    for slot in range(freqs):
        weight = frequency_weight(bins_ref, slot)
        weight_ref[slot] = jnp.full(weight_ref.shape[1:], 0.5 * weight * scale, jnp.float32)
        real, imag = green_s[slot, 0], green_s[slot, 1]
        slope_real = dot(table, real).astype(jnp.bfloat16)
        slope_imag = dot(table, imag).astype(jnp.bfloat16)
        near_real, near_imag = parts_of(green_r[slot])
        plain = dot(near_real, real) - dot(near_imag, imag)
        slope_x = dot(near_imag, slope_real[:cells]) + dot(near_real, slope_imag[:cells])
        slope_y = dot(near_imag, slope_real[cells:]) + dot(near_real, slope_imag[cells:])
        sound = sound + plain * (weight * weight * profile_ref[0] * scale)
        along_x = along_x + slope_x * (weight * scale)
        along_y = along_y + slope_y * (weight * scale)
    hot = hot_ref[...]
    for k, products in enumerate([sound, along_x, along_y]):
        out_ref[k] = pick_pairs(products, hot, receiver_ref)


def parts_of(rows):
    parts = jnp.swapaxes(rows, 0, 1)
    return parts[0], parts[1]


def layer_term(weight_ref, receiver_ref, hot, green_s, other_r):
    total = 0.0
    for slot in range(green_s.shape[0]):
        real, imag = parts_of(other_r[slot])
        both = dot(imag, green_s[slot, 0]) + dot(real, green_s[slot, 1])
        total = total + both * weight_ref[slot]
    return pick_pairs(total, hot, receiver_ref)


def near_term(weight_ref, receiver_ref, hot_ref, green_s, near_r, out_ref):
    out_ref[...] = layer_term(weight_ref, receiver_ref, hot_ref[...], green_s, near_r)


def far_term(
    share, weight_ref, receiver_ref, hot_ref, green_s, far_r, terms, near_ref, out_ref
):
    far = layer_term(weight_ref, receiver_ref, hot_ref[...], green_s, far_r)
    near = near_ref[...]
    odd = lax.rem(lax.axis_index("depth"), 2) == 1
    below = jnp.where(odd, near, far)
    above = jnp.where(odd, far, near)
    tiles = far.shape[0]
    group = lax.broadcasted_iota(jnp.int32, (tiles, LANES), 1) // share
    in_tile = LANES // share

    def moved(value, to, part):
        return pltpu.roll(value, (to - part) * share % LANES, 1) if to != part else value

    for part in range(in_tile):
        first = moved(below, 3, part)
        for k in range(3):
            first = jnp.where(group == k, moved(terms[k], k, part), first)
        out_ref[pl.ds(2 * part, tiles, stride=2 * in_tile), :] = first
        out_ref[pl.ds(2 * part + 1, tiles, stride=2 * in_tile), :] = moved(above, 0, part)


def combine(freqs, depths, share, parts_ref, out_ref):
    def row(which):
        total = parts_ref[pl.ds(which, depths, stride=2), :]
        for group in range(1, freqs):
            total = total + parts_ref[pl.ds(2 * group * depths + which, depths, stride=2), :]
        return total

    first = row(0)
    above = row(1)[:, :share]
    for k in range(3):
        out_ref[k] = first[:, k * share : (k + 1) * share]
    below = first[:, 3 * share : 4 * share]
    blank = jnp.zeros((1, share), jnp.float32)
    out_ref[3] = jnp.concatenate([below[1:], blank], axis=0) - jnp.concatenate(
        [blank, above[:-1]], axis=0
    )


def vmem(count):
    return [pl.BlockSpec(memory_space=pltpu.VMEM)] * count


def smem(count):
    return [pl.BlockSpec(memory_space=pltpu.SMEM)] * count


def on_device(
    green_source, green_receiver, source_index, receiver_index, frequency_bins, depth_profile
):
    local_freqs, _, sources, _, cells = green_source.shape
    receivers = green_receiver.shape[2]
    pairs = source_index.shape[0]
    n_freq, n_depth = lax.axis_size("freq"), lax.axis_size("depth")
    owners = n_freq * n_depth
    share = pairs // owners
    tiles = pairs // LANES
    scale = 1.0 / math.sqrt(2.0 * WX * WY * local_freqs * n_freq)
    params = pltpu.CompilerParams(vmem_limit_bytes=VMEM_BYTES)

    own = green_receiver[:, 0]
    paired = [(i, i ^ 1) for i in range(n_depth)]
    crossed = [(i, i + 1) for i in range(1, n_depth - 1, 2)]
    crossed += [(target, source) for source, target in crossed]
    everywhere = [
        (group * n_depth + source, group * n_depth + target)
        for group in range(n_freq)
        for source, target in crossed
    ]
    everywhere += [
        (group * n_depth + end, (group ^ 1) * n_depth + end)
        for group in range(n_freq)
        for end in (0, n_depth - 1)
    ]
    near_r = lax.ppermute(own, "depth", paired)
    far_r = lax.ppermute(own, ("freq", "depth"), everywhere)

    green_s = jnp.transpose(green_source[:, 0], (0, 2, 3, 1))
    source_row = source_index.reshape(1, pairs)
    receiver_row = receiver_index.reshape(1, pairs)
    product = 2 * 2 * cells * local_freqs * sources * receivers
    picking = 2 * 2 * sources * receivers * pairs

    def call(body, name, shapes, n_smem, n_vmem, terms):
        return pl.pallas_call(
            body,
            out_shape=shapes,
            in_specs=smem(n_smem) + vmem(n_vmem),
            out_specs=jax.tree.map(lambda _: pl.BlockSpec(memory_space=pltpu.VMEM), shapes),
            compiler_params=params,
            cost_estimate=pl.CostEstimate(
                flops=terms * (product + picking), bytes_accessed=1 << 21, transcendentals=0
            ),
            name=name,
        )

    term_shape = jax.ShapeDtypeStruct((tiles, LANES), jnp.float32)
    terms, hot, weights = call(
        functools.partial(local_terms, scale),
        "local_terms",
        [
            jax.ShapeDtypeStruct((3, tiles, LANES), jnp.float32),
            jax.ShapeDtypeStruct((sources, pairs), jnp.bfloat16),
            jax.ShapeDtypeStruct((local_freqs, 1, sources), jnp.float32),
        ],
        2, 4, 3,
    )(frequency_bins, depth_profile, source_row, receiver_row, green_s, own)
    near = call(near_term, "near_term", term_shape, 0, 5, 1)(
        weights, receiver_row, hot, green_s, near_r
    )
    parts = call(
        functools.partial(far_term, share),
        "far_term",
        jax.ShapeDtypeStruct((2 * owners, LANES), jnp.float32),
        0, 7, 1,
    )(weights, receiver_row, hot, green_s, far_r, terms, near)
    parts = lax.all_to_all(parts, ("freq", "depth"), split_axis=0, concat_axis=0, tiled=True)
    kernels = call(
        functools.partial(combine, n_freq, n_depth, share),
        "combine",
        jax.ShapeDtypeStruct((4, n_depth, share), jnp.float32),
        0, 1, 0,
    )(parts)
    return jnp.swapaxes(kernels, 1, 2)


def solution(mesh):
    placed = (
        P("freq", "depth", None, None, None),
        P("freq", "depth", None, None, None),
        P(),
        P(),
        P("freq"),
        P("depth"),
    )
    return jax.shard_map(
        on_device,
        mesh=mesh,
        in_specs=placed,
        out_specs=P(None, ("freq", "depth"), None),
        check_vma=False,
    )
```

```python
import functools
import math

import jax
import jax.numpy as jnp
from jax import lax
from jax.experimental import pallas as pl
from jax.experimental.pallas import tpu as pltpu
from jax.sharding import PartitionSpec as P

NBINS = 128
WX = 16
WY = 16
LANES = 128
VMEM_BYTES = 48 * 1024 * 1024


def dot(left, right):
    return jnp.dot(left, right, preferred_element_type=jnp.float32)


def frequency_weight(bins_ref, slot):
    return 0.5 + bins_ref[slot].astype(jnp.float32) / NBINS


def slope_table(cells):
    target = lax.broadcasted_iota(jnp.int32, (cells, cells), 0)
    source = lax.broadcasted_iota(jnp.int32, (cells, cells), 1)
    column = lax.rem(target, WY)
    step = source - target
    half, zero = jnp.float32(0.5), jnp.float32(0.0)
    along_x = jnp.where(step == WY, half, zero) - jnp.where(step == -WY, half, zero)
    along_y = jnp.where((step == 1) & (column != WY - 1), half, zero) - jnp.where(
        (step == -1) & (column != 0), half, zero
    )
    return jnp.concatenate([along_x, along_y], axis=0).astype(jnp.bfloat16)


def pick_sources(products, hot):
    receivers = products.shape[0]
    high = products.astype(jnp.bfloat16)
    low = (products - high.astype(jnp.float32)).astype(jnp.bfloat16)
    both = dot(jnp.concatenate([high, low], axis=0), hot)
    return both[:receivers] + both[receivers:]


def pick_receivers(picked, receiver_ref):
    receivers, pairs = picked.shape
    at_receiver = lax.broadcasted_iota(jnp.int32, (receivers, pairs), 0) == receiver_ref[...]
    row = jnp.sum(jnp.where(at_receiver, picked, 0.0), axis=0, keepdims=True)
    return jnp.concatenate(
        [row[:, at : at + LANES] for at in range(0, pairs, LANES)], axis=0
    )


def local_terms(
    scale,
    bins_ref,
    profile_ref,
    source_ref,
    receiver_ref,
    green_s,
    green_r,
    out_ref,
    column_ref,
    weight_ref,
):
    freqs, _, cells, sources = green_s.shape
    pairs = source_ref.shape[1]
    at_source = lax.broadcasted_iota(jnp.int32, (sources, pairs), 0) == source_ref[...]
    hot = jnp.where(at_source, jnp.float32(1), jnp.float32(0)).astype(jnp.bfloat16)
    table = slope_table(cells)
    sound = along_x = along_y = 0.0
    for slot in range(freqs):
        weight = frequency_weight(bins_ref, slot)
        weight_ref[slot] = jnp.full(weight_ref.shape[1:], 0.5 * weight * scale, jnp.float32)
        real, imag = green_s[slot, 0], green_s[slot, 1]
        column_ref[slot, 0] = dot(real, hot).astype(jnp.bfloat16)
        column_ref[slot, 1] = dot(imag, hot).astype(jnp.bfloat16)
        slope_real = dot(table, real).astype(jnp.bfloat16)
        slope_imag = dot(table, imag).astype(jnp.bfloat16)
        near_real, near_imag = parts_of(green_r[slot])
        plain = dot(near_real, real) - dot(near_imag, imag)
        slope_x = dot(near_imag, slope_real[:cells]) + dot(near_real, slope_imag[:cells])
        slope_y = dot(near_imag, slope_real[cells:]) + dot(near_real, slope_imag[cells:])
        sound = sound + plain * (weight * weight * profile_ref[0] * scale)
        along_x = along_x + slope_x * (weight * scale)
        along_y = along_y + slope_y * (weight * scale)
    for k, products in enumerate([sound, along_x, along_y]):
        out_ref[k] = pick_receivers(pick_sources(products, hot), receiver_ref)


def parts_of(rows):
    parts = jnp.swapaxes(rows, 0, 1)
    return parts[0], parts[1]


def layer_term(weight_ref, receiver_ref, column_ref, other_r):
    total = 0.0
    for slot in range(column_ref.shape[0]):
        real, imag = parts_of(other_r[slot])
        both = dot(imag, column_ref[slot, 0]) + dot(real, column_ref[slot, 1])
        total = total + both * weight_ref[slot]
    return pick_receivers(total, receiver_ref)


def near_term(weight_ref, receiver_ref, column_ref, near_r, out_ref):
    out_ref[...] = layer_term(weight_ref, receiver_ref, column_ref, near_r)


def far_term(
    share, weight_ref, receiver_ref, column_ref, far_r, terms, near_ref, out_ref
):
    far = layer_term(weight_ref, receiver_ref, column_ref, far_r)
    near = near_ref[...]
    odd = lax.rem(lax.axis_index("depth"), 2) == 1
    below = jnp.where(odd, near, far)
    above = jnp.where(odd, far, near)
    tiles = far.shape[0]
    group = lax.broadcasted_iota(jnp.int32, (tiles, LANES), 1) // share
    in_tile = LANES // share

    def moved(value, to, part):
        return pltpu.roll(value, (to - part) * share % LANES, 1) if to != part else value

    for part in range(in_tile):
        first = moved(below, 3, part)
        for k in range(3):
            first = jnp.where(group == k, moved(terms[k], k, part), first)
        out_ref[pl.ds(2 * part, tiles, stride=2 * in_tile), :] = first
        out_ref[pl.ds(2 * part + 1, tiles, stride=2 * in_tile), :] = moved(above, 0, part)


def combine(freqs, depths, share, parts_ref, out_ref):
    def row(which):
        total = parts_ref[pl.ds(which, depths, stride=2), :]
        for group in range(1, freqs):
            total = total + parts_ref[pl.ds(2 * group * depths + which, depths, stride=2), :]
        return total

    first = row(0)
    above = row(1)[:, :share]
    for k in range(3):
        out_ref[k] = first[:, k * share : (k + 1) * share]
    below = first[:, 3 * share : 4 * share]
    blank = jnp.zeros((1, share), jnp.float32)
    out_ref[3] = jnp.concatenate([below[1:], blank], axis=0) - jnp.concatenate(
        [blank, above[:-1]], axis=0
    )


def vmem(count):
    return [pl.BlockSpec(memory_space=pltpu.VMEM)] * count


def smem(count):
    return [pl.BlockSpec(memory_space=pltpu.SMEM)] * count


def on_device(
    green_source, green_receiver, source_index, receiver_index, frequency_bins, depth_profile
):
    local_freqs, _, sources, _, cells = green_source.shape
    receivers = green_receiver.shape[2]
    pairs = source_index.shape[0]
    n_freq, n_depth = lax.axis_size("freq"), lax.axis_size("depth")
    owners = n_freq * n_depth
    share = pairs // owners
    tiles = pairs // LANES
    scale = 1.0 / math.sqrt(2.0 * WX * WY * local_freqs * n_freq)
    params = pltpu.CompilerParams(vmem_limit_bytes=VMEM_BYTES)

    own = green_receiver[:, 0]
    paired = [(i, i ^ 1) for i in range(n_depth)]
    crossed = [(i, i + 1) for i in range(1, n_depth - 1, 2)]
    crossed += [(target, source) for source, target in crossed]
    everywhere = [
        (group * n_depth + source, group * n_depth + target)
        for group in range(n_freq)
        for source, target in crossed
    ]
    everywhere += [
        (group * n_depth + end, (group ^ 1) * n_depth + end)
        for group in range(n_freq)
        for end in (0, n_depth - 1)
    ]
    near_r = lax.ppermute(own, "depth", paired)
    far_r = lax.ppermute(own, ("freq", "depth"), everywhere)

    green_s = jnp.transpose(green_source[:, 0], (0, 2, 3, 1))
    source_row = source_index.reshape(1, pairs)
    receiver_row = receiver_index.reshape(1, pairs)
    product = 2 * 2 * cells * local_freqs * sources * receivers
    picking = 2 * 2 * sources * receivers * pairs

    def call(body, name, shapes, n_smem, n_vmem, terms):
        return pl.pallas_call(
            body,
            out_shape=shapes,
            in_specs=smem(n_smem) + vmem(n_vmem),
            out_specs=jax.tree.map(lambda _: pl.BlockSpec(memory_space=pltpu.VMEM), shapes),
            compiler_params=params,
            cost_estimate=pl.CostEstimate(
                flops=terms * (product + picking), bytes_accessed=1 << 21, transcendentals=0
            ),
            name=name,
        )

    term_shape = jax.ShapeDtypeStruct((tiles, LANES), jnp.float32)
    terms, columns, weights = call(
        functools.partial(local_terms, scale),
        "local_terms",
        [
            jax.ShapeDtypeStruct((3, tiles, LANES), jnp.float32),
            jax.ShapeDtypeStruct((local_freqs, 2, cells, pairs), jnp.bfloat16),
            jax.ShapeDtypeStruct((local_freqs, 1, pairs), jnp.float32),
        ],
        2, 4, 3,
    )(frequency_bins, depth_profile, source_row, receiver_row, green_s, own)
    near = call(near_term, "near_term", term_shape, 0, 4, 1)(
        weights, receiver_row, columns, near_r
    )
    parts = call(
        functools.partial(far_term, share),
        "far_term",
        jax.ShapeDtypeStruct((2 * owners, LANES), jnp.float32),
        0, 6, 1,
    )(weights, receiver_row, columns, far_r, terms, near)
    parts = lax.all_to_all(parts, ("freq", "depth"), split_axis=0, concat_axis=0, tiled=True)
    kernels = call(
        functools.partial(combine, n_freq, n_depth, share),
        "combine",
        jax.ShapeDtypeStruct((4, n_depth, share), jnp.float32),
        0, 1, 0,
    )(parts)
    return jnp.swapaxes(kernels, 1, 2)


def solution(mesh):
    placed = (
        P("freq", "depth", None, None, None),
        P("freq", "depth", None, None, None),
        P(),
        P(),
        P("freq"),
        P("depth"),
    )
    return jax.shard_map(
        on_device,
        mesh=mesh,
        in_specs=placed,
        out_specs=P(None, ("freq", "depth"), None),
        check_vma=False,
    )
```

```python
import functools
import math

import jax
import jax.numpy as jnp
from jax import lax
from jax.experimental import pallas as pl
from jax.experimental.pallas import tpu as pltpu
from jax.sharding import PartitionSpec as P

NBINS = 128
WX = 16
WY = 16
LANES = 128
VMEM_BYTES = 48 * 1024 * 1024


def dot(left, right):
    return jnp.dot(left, right, preferred_element_type=jnp.float32)


def frequency_weight(bins_ref, slot):
    return 0.5 + bins_ref[slot].astype(jnp.float32) / NBINS


def slope_table(cells):
    target = lax.broadcasted_iota(jnp.int32, (cells, cells), 0)
    source = lax.broadcasted_iota(jnp.int32, (cells, cells), 1)
    column = lax.rem(target, WY)
    step = source - target
    half, zero = jnp.float32(0.5), jnp.float32(0.0)
    along_x = jnp.where(step == WY, half, zero) - jnp.where(step == -WY, half, zero)
    along_y = jnp.where((step == 1) & (column != WY - 1), half, zero) - jnp.where(
        (step == -1) & (column != 0), half, zero
    )
    return jnp.concatenate([along_x, along_y], axis=0).astype(jnp.bfloat16)


def pick_sources(products, hot):
    receivers = products.shape[0]
    high = products.astype(jnp.bfloat16)
    low = (products - high.astype(jnp.float32)).astype(jnp.bfloat16)
    both = dot(jnp.concatenate([high, low], axis=0), hot)
    return both[:receivers] + both[receivers:]


def pick_receivers(picked, receiver_ref):
    receivers, pairs = picked.shape
    at_receiver = lax.broadcasted_iota(jnp.int32, (receivers, pairs), 0) == receiver_ref[...]
    row = jnp.sum(jnp.where(at_receiver, picked, 0.0), axis=0, keepdims=True)
    return jnp.concatenate(
        [row[:, at : at + LANES] for at in range(0, pairs, LANES)], axis=0
    )


def local_terms(
    scale,
    bins_ref,
    profile_ref,
    source_ref,
    receiver_ref,
    green_s,
    green_r,
    out_ref,
    column_ref,
    weight_ref,
):
    freqs, _, cells, sources = green_s.shape
    pairs = source_ref.shape[1]
    at_source = lax.broadcasted_iota(jnp.int32, (sources, pairs), 0) == source_ref[...]
    hot = jnp.where(at_source, jnp.float32(1), jnp.float32(0)).astype(jnp.bfloat16)
    table = slope_table(cells)
    sound = along_x = along_y = 0.0
    for slot in range(freqs):
        weight = frequency_weight(bins_ref, slot)
        weight_ref[slot] = jnp.full(weight_ref.shape[1:], 0.5 * weight * scale, jnp.float32)
        real, imag = green_s[slot, 0], green_s[slot, 1]
        column_ref[slot, 0] = dot(real, hot).astype(jnp.bfloat16)
        column_ref[slot, 1] = dot(imag, hot).astype(jnp.bfloat16)
        slope_real = dot(table, real).astype(jnp.bfloat16)
        slope_imag = dot(table, imag).astype(jnp.bfloat16)
        near_real, near_imag = parts_of(green_r[slot])
        plain = dot(near_real, real) - dot(near_imag, imag)
        slope_x = dot(near_imag, slope_real[:cells]) + dot(near_real, slope_imag[:cells])
        slope_y = dot(near_imag, slope_real[cells:]) + dot(near_real, slope_imag[cells:])
        sound = sound + plain * (weight * weight * profile_ref[0] * scale)
        along_x = along_x + slope_x * (weight * scale)
        along_y = along_y + slope_y * (weight * scale)
    for k, products in enumerate([sound, along_x, along_y]):
        out_ref[k] = pick_receivers(pick_sources(products, hot), receiver_ref)


def parts_of(rows):
    parts = jnp.swapaxes(rows, 0, 1)
    return parts[0], parts[1]


def layer_term(weight_ref, receiver_ref, column_ref, other_r):
    total = 0.0
    for slot in range(column_ref.shape[0]):
        real, imag = parts_of(other_r[slot])
        both = dot(imag, column_ref[slot, 0]) + dot(real, column_ref[slot, 1])
        total = total + both * weight_ref[slot]
    return pick_receivers(total, receiver_ref)


def near_term(weight_ref, receiver_ref, column_ref, near_r, out_ref):
    out_ref[...] = layer_term(weight_ref, receiver_ref, column_ref, near_r)


def far_term(
    share, weight_ref, receiver_ref, column_ref, far_r, terms, near_ref, out_ref
):
    far = layer_term(weight_ref, receiver_ref, column_ref, far_r)
    near = near_ref[...]
    odd = lax.rem(lax.axis_index("depth"), 2) == 1
    below = jnp.where(odd, near, far)
    above = jnp.where(odd, far, near)
    tiles = far.shape[0]
    group = lax.broadcasted_iota(jnp.int32, (tiles, LANES), 1) // share
    in_tile = LANES // share

    def moved(value, to, part):
        return pltpu.roll(value, (to - part) * share % LANES, 1) if to != part else value

    for part in range(in_tile):
        first = moved(below, 3, part)
        for k in range(3):
            first = jnp.where(group == k, moved(terms[k], k, part), first)
        out_ref[pl.ds(2 * part, tiles, stride=2 * in_tile), :] = first
        out_ref[pl.ds(2 * part + 1, tiles, stride=2 * in_tile), :] = moved(above, 0, part)


def combine(freqs, depths, share, parts_ref, out_ref):
    def row(which):
        total = parts_ref[pl.ds(which, depths, stride=2), :]
        for group in range(1, freqs):
            total = total + parts_ref[pl.ds(2 * group * depths + which, depths, stride=2), :]
        return total

    first, second = row(0), row(1)
    depth = lax.broadcasted_iota(jnp.int32, first.shape, 0)
    above = jnp.where(depth == depths - 1, 0.0, pltpu.roll(first, depths - 1, 0))
    below = jnp.where(depth == 0, 0.0, pltpu.roll(second, 1, 0))
    for k in range(3):
        out_ref[k] = pltpu.roll(first, (LANES - k * share) % LANES, 1)[:, :share]
    out_ref[3] = (pltpu.roll(above, LANES - 3 * share, 1) - below)[:, :share]


def vmem(count):
    return [pl.BlockSpec(memory_space=pltpu.VMEM)] * count


def smem(count):
    return [pl.BlockSpec(memory_space=pltpu.SMEM)] * count


def on_device(
    green_source, green_receiver, source_index, receiver_index, frequency_bins, depth_profile
):
    local_freqs, _, sources, _, cells = green_source.shape
    receivers = green_receiver.shape[2]
    pairs = source_index.shape[0]
    n_freq, n_depth = lax.axis_size("freq"), lax.axis_size("depth")
    owners = n_freq * n_depth
    share = pairs // owners
    tiles = pairs // LANES
    scale = 1.0 / math.sqrt(2.0 * WX * WY * local_freqs * n_freq)
    params = pltpu.CompilerParams(vmem_limit_bytes=VMEM_BYTES)

    own = green_receiver[:, 0]
    paired = [(i, i ^ 1) for i in range(n_depth)]
    crossed = [(i, i + 1) for i in range(1, n_depth - 1, 2)]
    crossed += [(target, source) for source, target in crossed]
    everywhere = [
        (group * n_depth + source, group * n_depth + target)
        for group in range(n_freq)
        for source, target in crossed
    ]
    everywhere += [
        (group * n_depth + end, (group ^ 1) * n_depth + end)
        for group in range(n_freq)
        for end in (0, n_depth - 1)
    ]
    near_r = lax.ppermute(own, "depth", paired)
    far_r = lax.ppermute(own, ("freq", "depth"), everywhere)

    green_s = jnp.transpose(green_source[:, 0], (0, 2, 3, 1))
    source_row = source_index.reshape(1, pairs)
    receiver_row = receiver_index.reshape(1, pairs)
    product = 2 * 2 * cells * local_freqs * sources * receivers
    picking = 2 * 2 * sources * receivers * pairs

    def call(body, name, shapes, n_smem, n_vmem, terms):
        return pl.pallas_call(
            body,
            out_shape=shapes,
            in_specs=smem(n_smem) + vmem(n_vmem),
            out_specs=jax.tree.map(lambda _: pl.BlockSpec(memory_space=pltpu.VMEM), shapes),
            compiler_params=params,
            cost_estimate=pl.CostEstimate(
                flops=terms * (product + picking), bytes_accessed=1 << 21, transcendentals=0
            ),
            name=name,
        )

    term_shape = jax.ShapeDtypeStruct((tiles, LANES), jnp.float32)
    terms, columns, weights = call(
        functools.partial(local_terms, scale),
        "local_terms",
        [
            jax.ShapeDtypeStruct((3, tiles, LANES), jnp.float32),
            jax.ShapeDtypeStruct((local_freqs, 2, cells, pairs), jnp.bfloat16),
            jax.ShapeDtypeStruct((local_freqs, 1, pairs), jnp.float32),
        ],
        2, 4, 3,
    )(frequency_bins, depth_profile, source_row, receiver_row, green_s, own)
    near = call(near_term, "near_term", term_shape, 0, 4, 1)(
        weights, receiver_row, columns, near_r
    )
    parts = call(
        functools.partial(far_term, share),
        "far_term",
        jax.ShapeDtypeStruct((2 * owners, LANES), jnp.float32),
        0, 6, 1,
    )(weights, receiver_row, columns, far_r, terms, near)
    parts = lax.all_to_all(parts, ("freq", "depth"), split_axis=0, concat_axis=0, tiled=True)
    kernels = call(
        functools.partial(combine, n_freq, n_depth, share),
        "combine",
        jax.ShapeDtypeStruct((4, n_depth, share), jnp.float32),
        0, 1, 0,
    )(parts)
    return jnp.swapaxes(kernels, 1, 2)


def solution(mesh):
    placed = (
        P("freq", "depth", None, None, None),
        P("freq", "depth", None, None, None),
        P(),
        P(),
        P("freq"),
        P("depth"),
    )
    return jax.shard_map(
        on_device,
        mesh=mesh,
        in_specs=placed,
        out_specs=P(None, ("freq", "depth"), None),
        check_vma=False,
    )
```

```python
import functools
import math

import jax
import jax.numpy as jnp
from jax import lax
from jax.experimental import pallas as pl
from jax.experimental.pallas import tpu as pltpu
from jax.sharding import PartitionSpec as P

NBINS = 128
WX = 16
WY = 16
LANES = 128
VMEM_BYTES = 48 * 1024 * 1024


def dot(left, right):
    return jnp.dot(left, right, preferred_element_type=jnp.float32)


def frequency_weight(bins_ref, slot):
    return 0.5 + bins_ref[slot].astype(jnp.float32) / NBINS


def slope_table(cells):
    target = lax.broadcasted_iota(jnp.int32, (cells, cells), 0)
    source = lax.broadcasted_iota(jnp.int32, (cells, cells), 1)
    column = lax.rem(target, WY)
    step = source - target
    half, zero = jnp.float32(0.5), jnp.float32(0.0)
    along_x = jnp.where(step == WY, half, zero) - jnp.where(step == -WY, half, zero)
    along_y = jnp.where((step == 1) & (column != WY - 1), half, zero) - jnp.where(
        (step == -1) & (column != 0), half, zero
    )
    return jnp.concatenate([along_x, along_y], axis=0).astype(jnp.bfloat16)


def pick_sources(products, hot):
    receivers = products.shape[0]
    high = products.astype(jnp.bfloat16)
    low = (products - high.astype(jnp.float32)).astype(jnp.bfloat16)
    both = dot(jnp.concatenate([high, low], axis=0), hot)
    return both[:receivers] + both[receivers:]


def pick_receivers(picked, receiver_ref):
    receivers, pairs = picked.shape
    at_receiver = lax.broadcasted_iota(jnp.int32, (receivers, pairs), 0) == receiver_ref[...]
    row = jnp.sum(jnp.where(at_receiver, picked, 0.0), axis=0, keepdims=True)
    return jnp.concatenate(
        [row[:, at : at + LANES] for at in range(0, pairs, LANES)], axis=0
    )


def local_terms(
    scale,
    bins_ref,
    profile_ref,
    source_ref,
    receiver_ref,
    green_s,
    green_r,
    out_ref,
    column_ref,
    weight_ref,
):
    freqs, _, cells, sources = green_s.shape
    pairs = source_ref.shape[1]
    at_source = lax.broadcasted_iota(jnp.int32, (sources, pairs), 0) == source_ref[...]
    hot = jnp.where(at_source, jnp.float32(1), jnp.float32(0)).astype(jnp.bfloat16)
    table = slope_table(cells)
    sound = along_x = along_y = 0.0
    for slot in range(freqs):
        weight = frequency_weight(bins_ref, slot)
        weight_ref[slot] = jnp.full(weight_ref.shape[1:], 0.5 * weight * scale, jnp.float32)
        real, imag = green_s[slot, 0], green_s[slot, 1]
        column_ref[slot, 0] = dot(real, hot).astype(jnp.bfloat16)
        column_ref[slot, 1] = dot(imag, hot).astype(jnp.bfloat16)
        slope_real = dot(table, real).astype(jnp.bfloat16)
        slope_imag = dot(table, imag).astype(jnp.bfloat16)
        near_real, near_imag = parts_of(green_r[slot])
        plain = dot(near_real, real) - dot(near_imag, imag)
        slope_x = dot(near_imag, slope_real[:cells]) + dot(near_real, slope_imag[:cells])
        slope_y = dot(near_imag, slope_real[cells:]) + dot(near_real, slope_imag[cells:])
        sound = sound + plain * (weight * weight * profile_ref[0] * scale)
        along_x = along_x + slope_x * (weight * scale)
        along_y = along_y + slope_y * (weight * scale)
    for k, products in enumerate([sound, along_x, along_y]):
        out_ref[k] = pick_receivers(pick_sources(products, hot), receiver_ref)


def parts_of(rows):
    parts = jnp.swapaxes(rows, 0, 1)
    return parts[0], parts[1]


def layer_term(weight_ref, receiver_ref, column_ref, other_r, first=0):
    total = 0.0
    for slot in range(first, first + other_r.shape[0]):
        real, imag = parts_of(other_r[slot - first])
        both = dot(imag, column_ref[slot, 0]) + dot(real, column_ref[slot, 1])
        total = total + both * weight_ref[slot]
    return pick_receivers(total, receiver_ref)


def near_term(weight_ref, receiver_ref, column_ref, near_r, out_ref):
    out_ref[...] = layer_term(weight_ref, receiver_ref, column_ref, near_r)


def far_term(
    share, weight_ref, receiver_ref, column_ref, far_r, terms, near_ref, half_ref, out_ref
):
    first = column_ref.shape[0] - far_r.shape[0]
    far = half_ref[...] + layer_term(weight_ref, receiver_ref, column_ref, far_r, first)
    near = near_ref[...]
    odd = lax.rem(lax.axis_index("depth"), 2) == 1
    below = jnp.where(odd, near, far)
    above = jnp.where(odd, far, near)
    tiles = far.shape[0]
    group = lax.broadcasted_iota(jnp.int32, (tiles, LANES), 1) // share
    in_tile = LANES // share

    def moved(value, to, part):
        return pltpu.roll(value, (to - part) * share % LANES, 1) if to != part else value

    for part in range(in_tile):
        first = moved(below, 3, part)
        for k in range(3):
            first = jnp.where(group == k, moved(terms[k], k, part), first)
        out_ref[pl.ds(2 * part, tiles, stride=2 * in_tile), :] = first
        out_ref[pl.ds(2 * part + 1, tiles, stride=2 * in_tile), :] = moved(above, 0, part)


def combine(freqs, depths, share, parts_ref, out_ref):
    def row(which):
        total = parts_ref[pl.ds(which, depths, stride=2), :]
        for group in range(1, freqs):
            total = total + parts_ref[pl.ds(2 * group * depths + which, depths, stride=2), :]
        return total

    first, second = row(0), row(1)
    depth = lax.broadcasted_iota(jnp.int32, first.shape, 0)
    above = jnp.where(depth == depths - 1, 0.0, pltpu.roll(first, depths - 1, 0))
    below = jnp.where(depth == 0, 0.0, pltpu.roll(second, 1, 0))
    for k in range(3):
        out_ref[k] = pltpu.roll(first, (LANES - k * share) % LANES, 1)[:, :share]
    out_ref[3] = (pltpu.roll(above, LANES - 3 * share, 1) - below)[:, :share]


def vmem(count):
    return [pl.BlockSpec(memory_space=pltpu.VMEM)] * count


def smem(count):
    return [pl.BlockSpec(memory_space=pltpu.SMEM)] * count


def on_device(
    green_source, green_receiver, source_index, receiver_index, frequency_bins, depth_profile
):
    local_freqs, _, sources, _, cells = green_source.shape
    receivers = green_receiver.shape[2]
    pairs = source_index.shape[0]
    n_freq, n_depth = lax.axis_size("freq"), lax.axis_size("depth")
    owners = n_freq * n_depth
    share = pairs // owners
    tiles = pairs // LANES
    scale = 1.0 / math.sqrt(2.0 * WX * WY * local_freqs * n_freq)
    params = pltpu.CompilerParams(vmem_limit_bytes=VMEM_BYTES)

    own = green_receiver[:, 0]
    paired = [(i, i ^ 1) for i in range(n_depth)]
    crossed = [(i, i + 1) for i in range(1, n_depth - 1, 2)]
    crossed += [(target, source) for source, target in crossed]
    everywhere = [
        (group * n_depth + source, group * n_depth + target)
        for group in range(n_freq)
        for source, target in crossed
    ]
    everywhere += [
        (group * n_depth + end, (group ^ 1) * n_depth + end)
        for group in range(n_freq)
        for end in (0, n_depth - 1)
    ]
    near_r = lax.ppermute(own, "depth", paired)
    half = local_freqs // 2
    far_a = lax.ppermute(own[:half], ("freq", "depth"), everywhere)
    far_b = lax.ppermute(own[half:], ("freq", "depth"), everywhere)

    green_s = jnp.transpose(green_source[:, 0], (0, 2, 3, 1))
    source_row = source_index.reshape(1, pairs)
    receiver_row = receiver_index.reshape(1, pairs)
    product = 2 * 2 * cells * local_freqs * sources * receivers
    picking = 2 * 2 * sources * receivers * pairs

    def call(body, name, shapes, n_smem, n_vmem, terms):
        return pl.pallas_call(
            body,
            out_shape=shapes,
            in_specs=smem(n_smem) + vmem(n_vmem),
            out_specs=jax.tree.map(lambda _: pl.BlockSpec(memory_space=pltpu.VMEM), shapes),
            compiler_params=params,
            cost_estimate=pl.CostEstimate(
                flops=int(terms * (product + picking)), bytes_accessed=1 << 21, transcendentals=0
            ),
            name=name,
        )

    term_shape = jax.ShapeDtypeStruct((tiles, LANES), jnp.float32)
    terms, columns, weights = call(
        functools.partial(local_terms, scale),
        "local_terms",
        [
            jax.ShapeDtypeStruct((3, tiles, LANES), jnp.float32),
            jax.ShapeDtypeStruct((local_freqs, 2, cells, pairs), jnp.bfloat16),
            jax.ShapeDtypeStruct((local_freqs, 1, pairs), jnp.float32),
        ],
        2, 4, 3,
    )(frequency_bins, depth_profile, source_row, receiver_row, green_s, own)
    near = call(near_term, "near_term", term_shape, 0, 4, 1)(
        weights, receiver_row, columns, near_r
    )
    halved = call(near_term, "half_term", term_shape, 0, 4, 0.5)(
        weights, receiver_row, columns, far_a
    )
    parts = call(
        functools.partial(far_term, share),
        "far_term",
        jax.ShapeDtypeStruct((2 * owners, LANES), jnp.float32),
        0, 7, 1,
    )(weights, receiver_row, columns, far_b, terms, near, halved)
    parts = lax.all_to_all(parts, ("freq", "depth"), split_axis=0, concat_axis=0, tiled=True)
    kernels = call(
        functools.partial(combine, n_freq, n_depth, share),
        "combine",
        jax.ShapeDtypeStruct((4, n_depth, share), jnp.float32),
        0, 1, 0,
    )(parts)
    return jnp.swapaxes(kernels, 1, 2)


def solution(mesh):
    placed = (
        P("freq", "depth", None, None, None),
        P("freq", "depth", None, None, None),
        P(),
        P(),
        P("freq"),
        P("depth"),
    )
    return jax.shard_map(
        on_device,
        mesh=mesh,
        in_specs=placed,
        out_specs=P(None, ("freq", "depth"), None),
        check_vma=False,
    )
```

```python
import functools
import math

import jax
import jax.numpy as jnp
from jax import lax
from jax.experimental import pallas as pl
from jax.experimental.pallas import tpu as pltpu
from jax.sharding import PartitionSpec as P

NBINS = 128
WX = 16
WY = 16
LANES = 128
VMEM_BYTES = 48 * 1024 * 1024


def dot(left, right):
    return jnp.dot(left, right, preferred_element_type=jnp.float32)


def frequency_weight(bins_ref, slot):
    return 0.5 + bins_ref[slot].astype(jnp.float32) / NBINS


def slope_table(cells):
    target = lax.broadcasted_iota(jnp.int32, (cells, cells), 0)
    source = lax.broadcasted_iota(jnp.int32, (cells, cells), 1)
    column = lax.rem(target, WY)
    step = source - target
    half, zero = jnp.float32(0.5), jnp.float32(0.0)
    along_x = jnp.where(step == WY, half, zero) - jnp.where(step == -WY, half, zero)
    along_y = jnp.where((step == 1) & (column != WY - 1), half, zero) - jnp.where(
        (step == -1) & (column != 0), half, zero
    )
    return jnp.concatenate([along_x, along_y], axis=0).astype(jnp.bfloat16)


def pick_sources(products, hot):
    receivers = products.shape[0]
    high = products.astype(jnp.bfloat16)
    low = (products - high.astype(jnp.float32)).astype(jnp.bfloat16)
    both = dot(jnp.concatenate([high, low], axis=0), hot)
    return both[:receivers] + both[receivers:]


def pick_receivers(picked, receiver_ref):
    receivers, pairs = picked.shape
    at_receiver = lax.broadcasted_iota(jnp.int32, (receivers, pairs), 0) == receiver_ref[...]
    row = jnp.sum(jnp.where(at_receiver, picked, 0.0), axis=0, keepdims=True)
    return jnp.concatenate(
        [row[:, at : at + LANES] for at in range(0, pairs, LANES)], axis=0
    )


def local_terms(
    scale,
    bins_ref,
    profile_ref,
    source_ref,
    receiver_ref,
    green_s,
    green_r,
    out_ref,
    column_ref,
    weight_ref,
):
    freqs, _, cells, sources = green_s.shape
    pairs = source_ref.shape[1]
    at_source = lax.broadcasted_iota(jnp.int32, (sources, pairs), 0) == source_ref[...]
    hot = jnp.where(at_source, jnp.float32(1), jnp.float32(0)).astype(jnp.bfloat16)
    table = slope_table(cells)
    sound = along_x = along_y = 0.0
    for slot in range(freqs):
        weight = frequency_weight(bins_ref, slot)
        weight_ref[slot] = jnp.full(weight_ref.shape[1:], 0.5 * weight * scale, jnp.float32)
        real, imag = green_s[slot, 0], green_s[slot, 1]
        column_ref[slot, 0] = dot(real, hot).astype(jnp.bfloat16)
        column_ref[slot, 1] = dot(imag, hot).astype(jnp.bfloat16)
        slope_real = dot(table, real).astype(jnp.bfloat16)
        slope_imag = dot(table, imag).astype(jnp.bfloat16)
        near_real, near_imag = parts_of(green_r[slot])
        plain = dot(near_real, real) - dot(near_imag, imag)
        slope_x = dot(near_imag, slope_real[:cells]) + dot(near_real, slope_imag[:cells])
        slope_y = dot(near_imag, slope_real[cells:]) + dot(near_real, slope_imag[cells:])
        sound = sound + plain * (weight * weight * profile_ref[0] * scale)
        along_x = along_x + slope_x * (weight * scale)
        along_y = along_y + slope_y * (weight * scale)
    for k, products in enumerate([sound, along_x, along_y]):
        out_ref[k] = pick_receivers(pick_sources(products, hot), receiver_ref)


def parts_of(rows):
    parts = jnp.swapaxes(rows, 0, 1)
    return parts[0], parts[1]


def layer_term(weight_ref, receiver_ref, column_ref, other_r, first=0):
    total = 0.0
    for slot in range(first, first + other_r.shape[0]):
        real, imag = parts_of(other_r[slot - first])
        both = dot(imag, column_ref[slot, 0]) + dot(real, column_ref[slot, 1])
        total = total + both * weight_ref[slot]
    return pick_receivers(total, receiver_ref)


def near_term(weight_ref, receiver_ref, column_ref, near_r, out_ref):
    out_ref[...] = layer_term(weight_ref, receiver_ref, column_ref, near_r)


def far_term(
    share, weight_ref, receiver_ref, column_ref, far_r, terms, near_ref, half_ref, out_ref
):
    first = column_ref.shape[0] - far_r.shape[0]
    far = half_ref[...] + layer_term(weight_ref, receiver_ref, column_ref, far_r, first)
    near = near_ref[...]
    odd = lax.rem(lax.axis_index("depth"), 2) == 1
    below = jnp.where(odd, far, near)
    above = jnp.where(odd, near, far)
    tiles = far.shape[0]
    group = lax.broadcasted_iota(jnp.int32, (tiles, LANES), 1) // share
    in_tile = LANES // share

    def moved(value, to, part):
        return pltpu.roll(value, (to - part) * share % LANES, 1) if to != part else value

    for part in range(in_tile):
        first = moved(below, 3, part)
        for k in range(3):
            first = jnp.where(group == k, moved(terms[k], k, part), first)
        out_ref[pl.ds(2 * part, tiles, stride=2 * in_tile), :] = first
        out_ref[pl.ds(2 * part + 1, tiles, stride=2 * in_tile), :] = moved(above, 0, part)


def combine(freqs, depths, share, parts_ref, out_ref):
    def row(which):
        total = parts_ref[pl.ds(which, depths, stride=2), :]
        for group in range(1, freqs):
            total = total + parts_ref[pl.ds(2 * group * depths + which, depths, stride=2), :]
        return total

    first, second = row(0), row(1)
    depth = lax.broadcasted_iota(jnp.int32, first.shape, 0)
    above = jnp.where(depth == depths - 1, 0.0, pltpu.roll(first, depths - 1, 0))
    below = jnp.where(depth == 0, 0.0, pltpu.roll(second, 1, 0))
    for k in range(3):
        out_ref[k] = pltpu.roll(first, (LANES - k * share) % LANES, 1)[:, :share]
    out_ref[3] = (pltpu.roll(above, LANES - 3 * share, 1) - below)[:, :share]


def vmem(count):
    return [pl.BlockSpec(memory_space=pltpu.VMEM)] * count


def smem(count):
    return [pl.BlockSpec(memory_space=pltpu.SMEM)] * count


def on_device(
    green_source, green_receiver, source_index, receiver_index, frequency_bins, depth_profile
):
    local_freqs, _, sources, _, cells = green_source.shape
    receivers = green_receiver.shape[2]
    pairs = source_index.shape[0]
    n_freq, n_depth = lax.axis_size("freq"), lax.axis_size("depth")
    owners = n_freq * n_depth
    share = pairs // owners
    tiles = pairs // LANES
    scale = 1.0 / math.sqrt(2.0 * WX * WY * local_freqs * n_freq)
    params = pltpu.CompilerParams(vmem_limit_bytes=VMEM_BYTES)

    own = green_receiver[:, 0]
    paired = [(i, i ^ 1) for i in range(n_depth)]
    crossed = [(i, i + 1) for i in range(1, n_depth - 1, 2)]
    crossed += [(target, source) for source, target in crossed]
    everywhere = [
        (group * n_depth + source, group * n_depth + target)
        for group in range(n_freq)
        for source, target in crossed
    ]
    everywhere += [
        (group * n_depth + end, (group ^ 1) * n_depth + end)
        for group in range(n_freq)
        for end in (0, n_depth - 1)
    ]
    half = local_freqs // 2
    far_r = lax.ppermute(own, ("freq", "depth"), everywhere)
    near_a = lax.ppermute(own[:half], "depth", paired)
    near_b = lax.ppermute(own[half:], "depth", paired)

    green_s = jnp.transpose(green_source[:, 0], (0, 2, 3, 1))
    source_row = source_index.reshape(1, pairs)
    receiver_row = receiver_index.reshape(1, pairs)
    product = 2 * 2 * cells * local_freqs * sources * receivers
    picking = 2 * 2 * sources * receivers * pairs

    def call(body, name, shapes, n_smem, n_vmem, terms):
        return pl.pallas_call(
            body,
            out_shape=shapes,
            in_specs=smem(n_smem) + vmem(n_vmem),
            out_specs=jax.tree.map(lambda _: pl.BlockSpec(memory_space=pltpu.VMEM), shapes),
            compiler_params=params,
            cost_estimate=pl.CostEstimate(
                flops=int(terms * (product + picking)), bytes_accessed=1 << 21, transcendentals=0
            ),
            name=name,
        )

    term_shape = jax.ShapeDtypeStruct((tiles, LANES), jnp.float32)
    terms, columns, weights = call(
        functools.partial(local_terms, scale),
        "local_terms",
        [
            jax.ShapeDtypeStruct((3, tiles, LANES), jnp.float32),
            jax.ShapeDtypeStruct((local_freqs, 2, cells, pairs), jnp.bfloat16),
            jax.ShapeDtypeStruct((local_freqs, 1, pairs), jnp.float32),
        ],
        2, 4, 3,
    )(frequency_bins, depth_profile, source_row, receiver_row, green_s, own)
    near = call(near_term, "near_term", term_shape, 0, 4, 1)(
        weights, receiver_row, columns, far_r
    )
    halved = call(near_term, "half_term", term_shape, 0, 4, 0.5)(
        weights, receiver_row, columns, near_a
    )
    parts = call(
        functools.partial(far_term, share),
        "far_term",
        jax.ShapeDtypeStruct((2 * owners, LANES), jnp.float32),
        0, 7, 1,
    )(weights, receiver_row, columns, near_b, terms, near, halved)
    parts = lax.all_to_all(parts, ("freq", "depth"), split_axis=0, concat_axis=0, tiled=True)
    kernels = call(
        functools.partial(combine, n_freq, n_depth, share),
        "combine",
        jax.ShapeDtypeStruct((4, n_depth, share), jnp.float32),
        0, 1, 0,
    )(parts)
    return jnp.swapaxes(kernels, 1, 2)


def solution(mesh):
    placed = (
        P("freq", "depth", None, None, None),
        P("freq", "depth", None, None, None),
        P(),
        P(),
        P("freq"),
        P("depth"),
    )
    return jax.shard_map(
        on_device,
        mesh=mesh,
        in_specs=placed,
        out_specs=P(None, ("freq", "depth"), None),
        check_vma=False,
    )
```

```python
import functools
import math

import jax
import jax.numpy as jnp
from jax import lax
from jax.experimental import pallas as pl
from jax.experimental.pallas import tpu as pltpu
from jax.sharding import PartitionSpec as P

NBINS = 128
WX = 16
WY = 16
LANES = 128
VMEM_BYTES = 48 * 1024 * 1024


def dot(left, right):
    return jnp.dot(left, right, preferred_element_type=jnp.float32)


def frequency_weight(bins_ref, slot):
    return 0.5 + bins_ref[slot].astype(jnp.float32) / NBINS


def slope_table(cells):
    target = lax.broadcasted_iota(jnp.int32, (cells, cells), 0)
    source = lax.broadcasted_iota(jnp.int32, (cells, cells), 1)
    column = lax.rem(target, WY)
    step = source - target
    half, zero = jnp.float32(0.5), jnp.float32(0.0)
    along_x = jnp.where(step == WY, half, zero) - jnp.where(step == -WY, half, zero)
    along_y = jnp.where((step == 1) & (column != WY - 1), half, zero) - jnp.where(
        (step == -1) & (column != 0), half, zero
    )
    return jnp.concatenate([along_x, along_y], axis=0).astype(jnp.bfloat16)


def pick_sources(products, hot):
    receivers = products.shape[0]
    high = products.astype(jnp.bfloat16)
    low = (products - high.astype(jnp.float32)).astype(jnp.bfloat16)
    both = dot(jnp.concatenate([high, low], axis=0), hot)
    return both[:receivers] + both[receivers:]


def pick_receivers(picked, receiver_ref):
    receivers, pairs = picked.shape
    at_receiver = lax.broadcasted_iota(jnp.int32, (receivers, pairs), 0) == receiver_ref[...]
    row = jnp.sum(jnp.where(at_receiver, picked, 0.0), axis=0, keepdims=True)
    return jnp.concatenate(
        [row[:, at : at + LANES] for at in range(0, pairs, LANES)], axis=0
    )


def local_terms(
    scale,
    bins_ref,
    profile_ref,
    source_ref,
    receiver_ref,
    green_s,
    green_r,
    out_ref,
    column_ref,
    weight_ref,
):
    freqs, _, cells, sources = green_s.shape
    pairs = source_ref.shape[1]
    at_source = lax.broadcasted_iota(jnp.int32, (sources, pairs), 0) == source_ref[...]
    hot = jnp.where(at_source, jnp.float32(1), jnp.float32(0)).astype(jnp.bfloat16)
    table = slope_table(cells)
    sound = along_x = along_y = 0.0
    for slot in range(freqs):
        weight = frequency_weight(bins_ref, slot)
        weight_ref[slot] = jnp.full(weight_ref.shape[1:], 0.5 * weight * scale, jnp.float32)
        real, imag = green_s[slot, 0], green_s[slot, 1]
        column_ref[slot, 0] = dot(real, hot).astype(jnp.bfloat16)
        column_ref[slot, 1] = dot(imag, hot).astype(jnp.bfloat16)
        slope_real = dot(table, real).astype(jnp.bfloat16)
        slope_imag = dot(table, imag).astype(jnp.bfloat16)
        near_real, near_imag = parts_of(green_r[slot])
        plain = dot(near_real, real) - dot(near_imag, imag)
        slope_x = dot(near_imag, slope_real[:cells]) + dot(near_real, slope_imag[:cells])
        slope_y = dot(near_imag, slope_real[cells:]) + dot(near_real, slope_imag[cells:])
        sound = sound + plain * (weight * weight * profile_ref[0] * scale)
        along_x = along_x + slope_x * (weight * scale)
        along_y = along_y + slope_y * (weight * scale)
    for k, products in enumerate([sound, along_x, along_y]):
        out_ref[k] = pick_receivers(pick_sources(products, hot), receiver_ref)


def parts_of(rows):
    parts = jnp.swapaxes(rows, 0, 1)
    return parts[0], parts[1]


def layer_term(weight_ref, receiver_ref, column_ref, other_r, first=0):
    total = 0.0
    for slot in range(first, first + other_r.shape[0]):
        real, imag = parts_of(other_r[slot - first])
        both = dot(imag, column_ref[slot, 0]) + dot(real, column_ref[slot, 1])
        total = total + both * weight_ref[slot]
    return pick_receivers(total, receiver_ref)


def half_term(weight_ref, receiver_ref, column_ref, near_r, out_ref):
    out_ref[...] = layer_term(weight_ref, receiver_ref, column_ref, near_r)


def moved(value, share, to, part):
    return pltpu.roll(value, (to - part) * share % LANES, 1) if to != part else value


def base_rows(share, weight_ref, receiver_ref, column_ref, near_r, terms, out_ref):
    near = layer_term(weight_ref, receiver_ref, column_ref, near_r)
    odd = lax.rem(lax.axis_index("depth"), 2) == 1
    below = jnp.where(odd, near, 0.0)
    above = jnp.where(odd, 0.0, near)
    tiles = near.shape[0]
    group = lax.broadcasted_iota(jnp.int32, (tiles, LANES), 1) // share
    in_tile = LANES // share
    for part in range(in_tile):
        first = moved(below, share, 3, part)
        for k in range(3):
            first = jnp.where(group == k, moved(terms[k], share, k, part), first)
        out_ref[part] = first
        out_ref[in_tile + part] = moved(above, share, 0, part)


def far_term(share, weight_ref, receiver_ref, column_ref, far_r, base, half_ref, out_ref):
    first = column_ref.shape[0] - far_r.shape[0]
    far = half_ref[...] + layer_term(weight_ref, receiver_ref, column_ref, far_r, first)
    odd = lax.rem(lax.axis_index("depth"), 2) == 1
    below = jnp.where(odd, 0.0, far)
    above = jnp.where(odd, far, 0.0)
    tiles = far.shape[0]
    last = lax.broadcasted_iota(jnp.int32, (tiles, LANES), 1) // share == 3
    in_tile = LANES // share
    for part in range(in_tile):
        own = jnp.where(last, moved(below, share, 3, part), 0.0)
        out_ref[pl.ds(2 * part, tiles, stride=2 * in_tile), :] = base[part] + own
        out_ref[pl.ds(2 * part + 1, tiles, stride=2 * in_tile), :] = base[
            in_tile + part
        ] + moved(above, share, 0, part)


def combine(freqs, depths, share, parts_ref, out_ref):
    def row(which):
        total = parts_ref[pl.ds(which, depths, stride=2), :]
        for group in range(1, freqs):
            total = total + parts_ref[pl.ds(2 * group * depths + which, depths, stride=2), :]
        return total

    first, second = row(0), row(1)
    depth = lax.broadcasted_iota(jnp.int32, first.shape, 0)
    above = jnp.where(depth == depths - 1, 0.0, pltpu.roll(first, depths - 1, 0))
    below = jnp.where(depth == 0, 0.0, pltpu.roll(second, 1, 0))
    for k in range(3):
        out_ref[k] = pltpu.roll(first, (LANES - k * share) % LANES, 1)[:, :share]
    out_ref[3] = (pltpu.roll(above, LANES - 3 * share, 1) - below)[:, :share]


def vmem(count):
    return [pl.BlockSpec(memory_space=pltpu.VMEM)] * count


def smem(count):
    return [pl.BlockSpec(memory_space=pltpu.SMEM)] * count


def on_device(
    green_source, green_receiver, source_index, receiver_index, frequency_bins, depth_profile
):
    local_freqs, _, sources, _, cells = green_source.shape
    receivers = green_receiver.shape[2]
    pairs = source_index.shape[0]
    n_freq, n_depth = lax.axis_size("freq"), lax.axis_size("depth")
    owners = n_freq * n_depth
    share = pairs // owners
    tiles = pairs // LANES
    scale = 1.0 / math.sqrt(2.0 * WX * WY * local_freqs * n_freq)
    params = pltpu.CompilerParams(vmem_limit_bytes=VMEM_BYTES)

    own = green_receiver[:, 0]
    paired = [(i, i ^ 1) for i in range(n_depth)]
    crossed = [(i, i + 1) for i in range(1, n_depth - 1, 2)]
    crossed += [(target, source) for source, target in crossed]
    everywhere = [
        (group * n_depth + source, group * n_depth + target)
        for group in range(n_freq)
        for source, target in crossed
    ]
    everywhere += [
        (group * n_depth + end, (group ^ 1) * n_depth + end)
        for group in range(n_freq)
        for end in (0, n_depth - 1)
    ]
    near_r = lax.ppermute(own, "depth", paired)
    half = local_freqs // 2
    far_a = lax.ppermute(own[:half], ("freq", "depth"), everywhere)
    far_b = lax.ppermute(own[half:], ("freq", "depth"), everywhere)

    green_s = jnp.transpose(green_source[:, 0], (0, 2, 3, 1))
    source_row = source_index.reshape(1, pairs)
    receiver_row = receiver_index.reshape(1, pairs)
    product = 2 * 2 * cells * local_freqs * sources * receivers
    picking = 2 * 2 * sources * receivers * pairs

    def call(body, name, shapes, n_smem, n_vmem, terms):
        return pl.pallas_call(
            body,
            out_shape=shapes,
            in_specs=smem(n_smem) + vmem(n_vmem),
            out_specs=jax.tree.map(lambda _: pl.BlockSpec(memory_space=pltpu.VMEM), shapes),
            compiler_params=params,
            cost_estimate=pl.CostEstimate(
                flops=int(terms * (product + picking)), bytes_accessed=1 << 21, transcendentals=0
            ),
            name=name,
        )

    term_shape = jax.ShapeDtypeStruct((tiles, LANES), jnp.float32)
    terms, columns, weights = call(
        functools.partial(local_terms, scale),
        "local_terms",
        [
            jax.ShapeDtypeStruct((3, tiles, LANES), jnp.float32),
            jax.ShapeDtypeStruct((local_freqs, 2, cells, pairs), jnp.bfloat16),
            jax.ShapeDtypeStruct((local_freqs, 1, pairs), jnp.float32),
        ],
        2, 4, 3,
    )(frequency_bins, depth_profile, source_row, receiver_row, green_s, own)
    base = call(
        functools.partial(base_rows, share),
        "base_rows",
        jax.ShapeDtypeStruct((2 * LANES // share, tiles, LANES), jnp.float32),
        0, 5, 1,
    )(weights, receiver_row, columns, near_r, terms)
    halved = call(half_term, "half_term", term_shape, 0, 4, 0.5)(
        weights, receiver_row, columns, far_a
    )
    parts = call(
        functools.partial(far_term, share),
        "far_term",
        jax.ShapeDtypeStruct((2 * owners, LANES), jnp.float32),
        0, 6, 1,
    )(weights, receiver_row, columns, far_b, base, halved)
    parts = lax.all_to_all(parts, ("freq", "depth"), split_axis=0, concat_axis=0, tiled=True)
    kernels = call(
        functools.partial(combine, n_freq, n_depth, share),
        "combine",
        jax.ShapeDtypeStruct((4, n_depth, share), jnp.float32),
        0, 1, 0,
    )(parts)
    return jnp.swapaxes(kernels, 1, 2)


def solution(mesh):
    placed = (
        P("freq", "depth", None, None, None),
        P("freq", "depth", None, None, None),
        P(),
        P(),
        P("freq"),
        P("depth"),
    )
    return jax.shard_map(
        on_device,
        mesh=mesh,
        in_specs=placed,
        out_specs=P(None, ("freq", "depth"), None),
        check_vma=False,
    )
```

```python
import functools
import math

import jax
import jax.numpy as jnp
from jax import lax
from jax.experimental import pallas as pl
from jax.experimental.pallas import tpu as pltpu
from jax.sharding import PartitionSpec as P

NBINS = 128
WX = 16
WY = 16
LANES = 128
VMEM_BYTES = 48 * 1024 * 1024


def dot(left, right):
    return jnp.dot(left, right, preferred_element_type=jnp.float32)


def frequency_weight(bins_ref, slot):
    return 0.5 + bins_ref[slot].astype(jnp.float32) / NBINS


def slope_table(cells):
    target = lax.broadcasted_iota(jnp.int32, (cells, cells), 0)
    source = lax.broadcasted_iota(jnp.int32, (cells, cells), 1)
    column = lax.rem(target, WY)
    step = source - target
    half, zero = jnp.float32(0.5), jnp.float32(0.0)
    along_x = jnp.where(step == WY, half, zero) - jnp.where(step == -WY, half, zero)
    along_y = jnp.where((step == 1) & (column != WY - 1), half, zero) - jnp.where(
        (step == -1) & (column != 0), half, zero
    )
    return jnp.concatenate([along_x, along_y], axis=0).astype(jnp.bfloat16)


def pick_sources(products, hot):
    receivers = products.shape[0]
    high = products.astype(jnp.bfloat16)
    low = (products - high.astype(jnp.float32)).astype(jnp.bfloat16)
    both = dot(jnp.concatenate([high, low], axis=0), hot)
    return both[:receivers] + both[receivers:]


def pick_receivers(picked, receiver_ref):
    receivers, pairs = picked.shape
    at_receiver = lax.broadcasted_iota(jnp.int32, (receivers, pairs), 0) == receiver_ref[...]
    row = jnp.sum(jnp.where(at_receiver, picked, 0.0), axis=0, keepdims=True)
    return jnp.concatenate(
        [row[:, at : at + LANES] for at in range(0, pairs, LANES)], axis=0
    )


def local_terms(
    scale,
    bins_ref,
    profile_ref,
    source_ref,
    receiver_ref,
    green_s,
    green_r,
    out_ref,
    column_ref,
    weight_ref,
):
    freqs, _, cells, sources = green_s.shape
    pairs = source_ref.shape[1]
    at_source = lax.broadcasted_iota(jnp.int32, (sources, pairs), 0) == source_ref[...]
    hot = jnp.where(at_source, jnp.float32(1), jnp.float32(0)).astype(jnp.bfloat16)
    table = slope_table(cells)
    sound = along_x = along_y = 0.0
    for slot in range(freqs):
        weight = frequency_weight(bins_ref, slot)
        weight_ref[slot] = jnp.full(weight_ref.shape[1:], 0.5 * weight * scale, jnp.float32)
        real, imag = green_s[slot, 0], green_s[slot, 1]
        column_ref[slot, 0] = dot(real, hot).astype(jnp.bfloat16)
        column_ref[slot, 1] = dot(imag, hot).astype(jnp.bfloat16)
        slope_real = dot(table, real).astype(jnp.bfloat16)
        slope_imag = dot(table, imag).astype(jnp.bfloat16)
        near_real, near_imag = parts_of(green_r[slot])
        plain = dot(near_real, real) - dot(near_imag, imag)
        slope_x = dot(near_imag, slope_real[:cells]) + dot(near_real, slope_imag[:cells])
        slope_y = dot(near_imag, slope_real[cells:]) + dot(near_real, slope_imag[cells:])
        sound = sound + plain * (weight * weight * profile_ref[0] * scale)
        along_x = along_x + slope_x * (weight * scale)
        along_y = along_y + slope_y * (weight * scale)
    for k, products in enumerate([sound, along_x, along_y]):
        out_ref[k] = pick_receivers(pick_sources(products, hot), receiver_ref)


def parts_of(rows):
    parts = jnp.swapaxes(rows, 0, 1)
    return parts[0], parts[1]


def layer_term(weight_ref, receiver_ref, column_ref, other_r, first=0):
    total = 0.0
    for slot in range(first, first + other_r.shape[0]):
        real, imag = parts_of(other_r[slot - first])
        both = dot(imag, column_ref[slot, 0]) + dot(real, column_ref[slot, 1])
        total = total + both * weight_ref[slot]
    return pick_receivers(total, receiver_ref)


def half_term(weight_ref, receiver_ref, column_ref, near_r, out_ref):
    out_ref[...] = layer_term(weight_ref, receiver_ref, column_ref, near_r)


def moved(value, share, to, part):
    return pltpu.roll(value, (to - part) * share % LANES, 1) if to != part else value


def base_rows(share, weight_ref, receiver_ref, column_ref, near_r, terms, out_ref):
    near = layer_term(weight_ref, receiver_ref, column_ref, near_r)
    odd = lax.rem(lax.axis_index("depth"), 2) == 1
    below = jnp.where(odd, 0.0, near)
    above = jnp.where(odd, near, 0.0)
    tiles = near.shape[0]
    group = lax.broadcasted_iota(jnp.int32, (tiles, LANES), 1) // share
    in_tile = LANES // share
    for part in range(in_tile):
        first = moved(below, share, 3, part)
        for k in range(3):
            first = jnp.where(group == k, moved(terms[k], share, k, part), first)
        out_ref[part] = first
        out_ref[in_tile + part] = moved(above, share, 0, part)


def far_term(share, weight_ref, receiver_ref, column_ref, far_r, base, half_ref, out_ref):
    first = column_ref.shape[0] - far_r.shape[0]
    far = half_ref[...] + layer_term(weight_ref, receiver_ref, column_ref, far_r, first)
    odd = lax.rem(lax.axis_index("depth"), 2) == 1
    below = jnp.where(odd, far, 0.0)
    above = jnp.where(odd, 0.0, far)
    tiles = far.shape[0]
    last = lax.broadcasted_iota(jnp.int32, (tiles, LANES), 1) // share == 3
    in_tile = LANES // share
    for part in range(in_tile):
        own = jnp.where(last, moved(below, share, 3, part), 0.0)
        out_ref[pl.ds(2 * part, tiles, stride=2 * in_tile), :] = base[part] + own
        out_ref[pl.ds(2 * part + 1, tiles, stride=2 * in_tile), :] = base[
            in_tile + part
        ] + moved(above, share, 0, part)


def combine(freqs, depths, share, parts_ref, out_ref):
    def row(which):
        total = parts_ref[pl.ds(which, depths, stride=2), :]
        for group in range(1, freqs):
            total = total + parts_ref[pl.ds(2 * group * depths + which, depths, stride=2), :]
        return total

    first, second = row(0), row(1)
    depth = lax.broadcasted_iota(jnp.int32, first.shape, 0)
    above = jnp.where(depth == depths - 1, 0.0, pltpu.roll(first, depths - 1, 0))
    below = jnp.where(depth == 0, 0.0, pltpu.roll(second, 1, 0))
    for k in range(3):
        out_ref[k] = pltpu.roll(first, (LANES - k * share) % LANES, 1)[:, :share]
    out_ref[3] = (pltpu.roll(above, LANES - 3 * share, 1) - below)[:, :share]


def vmem(count):
    return [pl.BlockSpec(memory_space=pltpu.VMEM)] * count


def smem(count):
    return [pl.BlockSpec(memory_space=pltpu.SMEM)] * count


def on_device(
    green_source, green_receiver, source_index, receiver_index, frequency_bins, depth_profile
):
    local_freqs, _, sources, _, cells = green_source.shape
    receivers = green_receiver.shape[2]
    pairs = source_index.shape[0]
    n_freq, n_depth = lax.axis_size("freq"), lax.axis_size("depth")
    owners = n_freq * n_depth
    share = pairs // owners
    tiles = pairs // LANES
    scale = 1.0 / math.sqrt(2.0 * WX * WY * local_freqs * n_freq)
    params = pltpu.CompilerParams(vmem_limit_bytes=VMEM_BYTES)

    own = green_receiver[:, 0]
    paired = [(i, i ^ 1) for i in range(n_depth)]
    crossed = [(i, i + 1) for i in range(1, n_depth - 1, 2)]
    crossed += [(target, source) for source, target in crossed]
    everywhere = [
        (group * n_depth + source, group * n_depth + target)
        for group in range(n_freq)
        for source, target in crossed
    ]
    everywhere += [
        (group * n_depth + end, (group ^ 1) * n_depth + end)
        for group in range(n_freq)
        for end in (0, n_depth - 1)
    ]
    half = local_freqs // 2
    far_r = lax.ppermute(own, ("freq", "depth"), everywhere)
    near_a = lax.ppermute(own[:half], "depth", paired)
    near_b = lax.ppermute(own[half:], "depth", paired)

    green_s = jnp.transpose(green_source[:, 0], (0, 2, 3, 1))
    source_row = source_index.reshape(1, pairs)
    receiver_row = receiver_index.reshape(1, pairs)
    product = 2 * 2 * cells * local_freqs * sources * receivers
    picking = 2 * 2 * sources * receivers * pairs

    def call(body, name, shapes, n_smem, n_vmem, terms):
        return pl.pallas_call(
            body,
            out_shape=shapes,
            in_specs=smem(n_smem) + vmem(n_vmem),
            out_specs=jax.tree.map(lambda _: pl.BlockSpec(memory_space=pltpu.VMEM), shapes),
            compiler_params=params,
            cost_estimate=pl.CostEstimate(
                flops=int(terms * (product + picking)), bytes_accessed=1 << 21, transcendentals=0
            ),
            name=name,
        )

    term_shape = jax.ShapeDtypeStruct((tiles, LANES), jnp.float32)
    terms, columns, weights = call(
        functools.partial(local_terms, scale),
        "local_terms",
        [
            jax.ShapeDtypeStruct((3, tiles, LANES), jnp.float32),
            jax.ShapeDtypeStruct((local_freqs, 2, cells, pairs), jnp.bfloat16),
            jax.ShapeDtypeStruct((local_freqs, 1, pairs), jnp.float32),
        ],
        2, 4, 3,
    )(frequency_bins, depth_profile, source_row, receiver_row, green_s, own)
    base = call(
        functools.partial(base_rows, share),
        "base_rows",
        jax.ShapeDtypeStruct((2 * LANES // share, tiles, LANES), jnp.float32),
        0, 5, 1,
    )(weights, receiver_row, columns, far_r, terms)
    halved = call(half_term, "half_term", term_shape, 0, 4, 0.5)(
        weights, receiver_row, columns, near_a
    )
    parts = call(
        functools.partial(far_term, share),
        "far_term",
        jax.ShapeDtypeStruct((2 * owners, LANES), jnp.float32),
        0, 6, 1,
    )(weights, receiver_row, columns, near_b, base, halved)
    parts = lax.all_to_all(parts, ("freq", "depth"), split_axis=0, concat_axis=0, tiled=True)
    kernels = call(
        functools.partial(combine, n_freq, n_depth, share),
        "combine",
        jax.ShapeDtypeStruct((4, n_depth, share), jnp.float32),
        0, 1, 0,
    )(parts)
    return jnp.swapaxes(kernels, 1, 2)


def solution(mesh):
    placed = (
        P("freq", "depth", None, None, None),
        P("freq", "depth", None, None, None),
        P(),
        P(),
        P("freq"),
        P("depth"),
    )
    return jax.shard_map(
        on_device,
        mesh=mesh,
        in_specs=placed,
        out_specs=P(None, ("freq", "depth"), None),
        check_vma=False,
    )
```

```python
import functools
import math

import jax
import jax.numpy as jnp
from jax import lax
from jax.experimental import pallas as pl
from jax.experimental.pallas import tpu as pltpu
from jax.sharding import PartitionSpec as P

NBINS = 128
WX = 16
WY = 16
LANES = 128
VMEM_BYTES = 48 * 1024 * 1024


def dot(left, right):
    return jnp.dot(left, right, preferred_element_type=jnp.float32)


def frequency_weight(bins_ref, slot):
    return 0.5 + bins_ref[slot].astype(jnp.float32) / NBINS


def slope_table(cells):
    target = lax.broadcasted_iota(jnp.int32, (cells, cells), 0)
    source = lax.broadcasted_iota(jnp.int32, (cells, cells), 1)
    column = lax.rem(target, WY)
    step = source - target
    half, zero = jnp.float32(0.5), jnp.float32(0.0)
    along_x = jnp.where(step == WY, half, zero) - jnp.where(step == -WY, half, zero)
    along_y = jnp.where((step == 1) & (column != WY - 1), half, zero) - jnp.where(
        (step == -1) & (column != 0), half, zero
    )
    return jnp.concatenate([along_x, along_y], axis=0).astype(jnp.bfloat16)


def pick_sources(products, hot):
    receivers = products.shape[0]
    high = products.astype(jnp.bfloat16)
    low = (products - high.astype(jnp.float32)).astype(jnp.bfloat16)
    both = dot(jnp.concatenate([high, low], axis=0), hot)
    return both[:receivers] + both[receivers:]


def pick_receivers(picked, receiver_ref):
    receivers, pairs = picked.shape
    at_receiver = lax.broadcasted_iota(jnp.int32, (receivers, pairs), 0) == receiver_ref[...]
    row = jnp.sum(jnp.where(at_receiver, picked, 0.0), axis=0, keepdims=True)
    return jnp.concatenate(
        [row[:, at : at + LANES] for at in range(0, pairs, LANES)], axis=0
    )


def local_terms(
    scale,
    bins_ref,
    profile_ref,
    source_ref,
    receiver_ref,
    green_s,
    green_r,
    out_ref,
    column_ref,
    weight_ref,
):
    freqs, _, cells, sources = green_s.shape
    pairs = source_ref.shape[1]
    at_source = lax.broadcasted_iota(jnp.int32, (sources, pairs), 0) == source_ref[...]
    hot = jnp.where(at_source, jnp.float32(1), jnp.float32(0)).astype(jnp.bfloat16)
    table = slope_table(cells)
    sound = along_x = along_y = 0.0
    for slot in range(freqs):
        weight = frequency_weight(bins_ref, slot)
        weight_ref[slot] = jnp.full(weight_ref.shape[1:], 0.5 * weight * scale, jnp.float32)
        real, imag = green_s[slot, 0], green_s[slot, 1]
        column_ref[slot, 0] = dot(real, hot).astype(jnp.bfloat16)
        column_ref[slot, 1] = dot(imag, hot).astype(jnp.bfloat16)
        slope_real = dot(table, real).astype(jnp.bfloat16)
        slope_imag = dot(table, imag).astype(jnp.bfloat16)
        near_real, near_imag = parts_of(green_r[slot])
        plain = dot(near_real, real) - dot(near_imag, imag)
        slope_x = dot(near_imag, slope_real[:cells]) + dot(near_real, slope_imag[:cells])
        slope_y = dot(near_imag, slope_real[cells:]) + dot(near_real, slope_imag[cells:])
        sound = sound + plain * (weight * weight * profile_ref[0] * scale)
        along_x = along_x + slope_x * (weight * scale)
        along_y = along_y + slope_y * (weight * scale)
    for k, products in enumerate([sound, along_x, along_y]):
        out_ref[k] = pick_receivers(pick_sources(products, hot), receiver_ref)


def parts_of(rows):
    parts = jnp.swapaxes(rows, 0, 1)
    return parts[0], parts[1]


def layer_term(weight_ref, receiver_ref, column_ref, other_r, first=0):
    total = 0.0
    for slot in range(first, first + other_r.shape[0]):
        real, imag = parts_of(other_r[slot - first])
        both = dot(imag, column_ref[slot, 0]) + dot(real, column_ref[slot, 1])
        total = total + (both * weight_ref[slot] if other_r.shape[0] > 1 else both)
    picked = pick_receivers(total, receiver_ref)
    return picked if other_r.shape[0] > 1 else picked * weight_ref[first, :, :LANES]


def half_term(weight_ref, receiver_ref, column_ref, near_r, out_ref):
    out_ref[...] = layer_term(weight_ref, receiver_ref, column_ref, near_r)


def moved(value, share, to, part):
    return pltpu.roll(value, (to - part) * share % LANES, 1) if to != part else value


def base_rows(share, weight_ref, receiver_ref, column_ref, far_r, terms, out_ref):
    far = layer_term(weight_ref, receiver_ref, column_ref, far_r)
    odd = lax.rem(lax.axis_index("depth"), 2) == 1
    below = jnp.where(odd, 0.0, far)
    above = jnp.where(odd, far, 0.0)
    tiles = far.shape[0]
    group = lax.broadcasted_iota(jnp.int32, (tiles, LANES), 1) // share
    in_tile = LANES // share
    for part in range(in_tile):
        first = moved(below, share, 3, part)
        for k in range(3):
            first = jnp.where(group == k, moved(terms[k], share, k, part), first)
        out_ref[part] = first
        out_ref[in_tile + part] = moved(above, share, 0, part)


def near_term(share, weight_ref, receiver_ref, column_ref, near_r, base, half_ref, out_ref):
    first = column_ref.shape[0] - near_r.shape[0]
    near = half_ref[...] + layer_term(weight_ref, receiver_ref, column_ref, near_r, first)
    odd = lax.rem(lax.axis_index("depth"), 2) == 1
    below = jnp.where(odd, near, 0.0)
    above = jnp.where(odd, 0.0, near)
    tiles = near.shape[0]
    last = lax.broadcasted_iota(jnp.int32, (tiles, LANES), 1) // share == 3
    in_tile = LANES // share
    for part in range(in_tile):
        own = jnp.where(last, moved(below, share, 3, part), 0.0)
        out_ref[pl.ds(2 * part, tiles, stride=2 * in_tile), :] = base[part] + own
        out_ref[pl.ds(2 * part + 1, tiles, stride=2 * in_tile), :] = base[
            in_tile + part
        ] + moved(above, share, 0, part)


def combine(freqs, depths, share, parts_ref, out_ref):
    def row(which):
        total = parts_ref[pl.ds(which, depths, stride=2), :]
        for group in range(1, freqs):
            total = total + parts_ref[pl.ds(2 * group * depths + which, depths, stride=2), :]
        return total

    first, second = row(0), row(1)
    depth = lax.broadcasted_iota(jnp.int32, first.shape, 0)
    above = jnp.where(depth == depths - 1, 0.0, pltpu.roll(first, depths - 1, 0))
    below = jnp.where(depth == 0, 0.0, pltpu.roll(second, 1, 0))
    for k in range(3):
        out_ref[k] = pltpu.roll(first, (LANES - k * share) % LANES, 1)[:, :share]
    out_ref[3] = (pltpu.roll(above, LANES - 3 * share, 1) - below)[:, :share]


def vmem(count):
    return [pl.BlockSpec(memory_space=pltpu.VMEM)] * count


def smem(count):
    return [pl.BlockSpec(memory_space=pltpu.SMEM)] * count


def on_device(
    green_source, green_receiver, source_index, receiver_index, frequency_bins, depth_profile
):
    local_freqs, _, sources, _, cells = green_source.shape
    receivers = green_receiver.shape[2]
    pairs = source_index.shape[0]
    n_freq, n_depth = lax.axis_size("freq"), lax.axis_size("depth")
    owners = n_freq * n_depth
    share = pairs // owners
    tiles = pairs // LANES
    scale = 1.0 / math.sqrt(2.0 * WX * WY * local_freqs * n_freq)
    params = pltpu.CompilerParams(vmem_limit_bytes=VMEM_BYTES)

    own = green_receiver[:, 0]
    paired = [(i, i ^ 1) for i in range(n_depth)]
    crossed = [(i, i + 1) for i in range(1, n_depth - 1, 2)]
    crossed += [(target, source) for source, target in crossed]
    everywhere = [
        (group * n_depth + source, group * n_depth + target)
        for group in range(n_freq)
        for source, target in crossed
    ]
    everywhere += [
        (group * n_depth + end, (group ^ 1) * n_depth + end)
        for group in range(n_freq)
        for end in (0, n_depth - 1)
    ]
    half = local_freqs // 2
    far_r = lax.ppermute(own, ("freq", "depth"), everywhere)
    near_a = lax.ppermute(own[:half], "depth", paired)
    near_b = lax.ppermute(own[half:], "depth", paired)

    green_s = jnp.transpose(green_source[:, 0], (0, 2, 3, 1))
    source_row = source_index.reshape(1, pairs)
    receiver_row = receiver_index.reshape(1, pairs)
    product = 2 * 2 * cells * local_freqs * sources * receivers
    picking = 2 * 2 * sources * receivers * pairs

    def call(body, name, shapes, n_smem, n_vmem, terms):
        return pl.pallas_call(
            body,
            out_shape=shapes,
            in_specs=smem(n_smem) + vmem(n_vmem),
            out_specs=jax.tree.map(lambda _: pl.BlockSpec(memory_space=pltpu.VMEM), shapes),
            compiler_params=params,
            cost_estimate=pl.CostEstimate(
                flops=int(terms * (product + picking)), bytes_accessed=1 << 21, transcendentals=0
            ),
            name=name,
        )

    term_shape = jax.ShapeDtypeStruct((tiles, LANES), jnp.float32)
    terms, columns, weights = call(
        functools.partial(local_terms, scale),
        "local_terms",
        [
            jax.ShapeDtypeStruct((3, tiles, LANES), jnp.float32),
            jax.ShapeDtypeStruct((local_freqs, 2, cells, pairs), jnp.bfloat16),
            jax.ShapeDtypeStruct((local_freqs, 1, pairs), jnp.float32),
        ],
        2, 4, 3,
    )(frequency_bins, depth_profile, source_row, receiver_row, green_s, own)
    base = call(
        functools.partial(base_rows, share),
        "base_rows",
        jax.ShapeDtypeStruct((2 * LANES // share, tiles, LANES), jnp.float32),
        0, 5, 1,
    )(weights, receiver_row, columns, far_r, terms)
    halved = call(half_term, "half_term", term_shape, 0, 4, 0.5)(
        weights, receiver_row, columns, near_a
    )
    parts = call(
        functools.partial(near_term, share),
        "near_term",
        jax.ShapeDtypeStruct((2 * owners, LANES), jnp.float32),
        0, 6, 1,
    )(weights, receiver_row, columns, near_b, base, halved)
    parts = lax.all_to_all(parts, ("freq", "depth"), split_axis=0, concat_axis=0, tiled=True)
    kernels = call(
        functools.partial(combine, n_freq, n_depth, share),
        "combine",
        jax.ShapeDtypeStruct((4, n_depth, share), jnp.float32),
        0, 1, 0,
    )(parts)
    return jnp.swapaxes(kernels, 1, 2)


def solution(mesh):
    placed = (
        P("freq", "depth", None, None, None),
        P("freq", "depth", None, None, None),
        P(),
        P(),
        P("freq"),
        P("depth"),
    )
    return jax.shard_map(
        on_device,
        mesh=mesh,
        in_specs=placed,
        out_specs=P(None, ("freq", "depth"), None),
        check_vma=False,
    )
```

```python
import functools
import math

import jax
import jax.numpy as jnp
from jax import lax
from jax.experimental import pallas as pl
from jax.experimental.pallas import tpu as pltpu
from jax.sharding import PartitionSpec as P

NBINS = 128
WX = 16
WY = 16
LANES = 128
VMEM_BYTES = 24 * 1024 * 1024


def dot(left, right):
    return jnp.dot(left, right, preferred_element_type=jnp.float32)


def frequency_weight(bins_ref, slot):
    return 0.5 + bins_ref[slot].astype(jnp.float32) / NBINS


def slope_table(cells):
    target = lax.broadcasted_iota(jnp.int32, (cells, cells), 0)
    source = lax.broadcasted_iota(jnp.int32, (cells, cells), 1)
    column = lax.rem(target, WY)
    step = source - target
    half, zero = jnp.float32(0.5), jnp.float32(0.0)
    along_x = jnp.where(step == WY, half, zero) - jnp.where(step == -WY, half, zero)
    along_y = jnp.where((step == 1) & (column != WY - 1), half, zero) - jnp.where(
        (step == -1) & (column != 0), half, zero
    )
    return jnp.concatenate([along_x, along_y], axis=0).astype(jnp.bfloat16)


def pick_sources(products, hot):
    receivers = products.shape[0]
    high = products.astype(jnp.bfloat16)
    low = (products - high.astype(jnp.float32)).astype(jnp.bfloat16)
    both = dot(jnp.concatenate([high, low], axis=0), hot)
    return both[:receivers] + both[receivers:]


def pick_receivers(picked, receiver_ref):
    receivers, pairs = picked.shape
    at_receiver = lax.broadcasted_iota(jnp.int32, (receivers, pairs), 0) == receiver_ref[...]
    row = jnp.sum(jnp.where(at_receiver, picked, 0.0), axis=0, keepdims=True)
    return jnp.concatenate(
        [row[:, at : at + LANES] for at in range(0, pairs, LANES)], axis=0
    )


def local_terms(
    scale,
    bins_ref,
    profile_ref,
    source_ref,
    receiver_ref,
    green_s,
    green_r,
    out_ref,
    column_ref,
    weight_ref,
):
    freqs, _, cells, sources = green_s.shape
    pairs = source_ref.shape[1]
    at_source = lax.broadcasted_iota(jnp.int32, (sources, pairs), 0) == source_ref[...]
    hot = jnp.where(at_source, jnp.float32(1), jnp.float32(0)).astype(jnp.bfloat16)
    table = slope_table(cells)
    sound = along_x = along_y = 0.0
    for slot in range(freqs):
        weight = frequency_weight(bins_ref, slot)
        weight_ref[slot] = jnp.full(weight_ref.shape[1:], 0.5 * weight * scale, jnp.float32)
        real, imag = green_s[slot, 0], green_s[slot, 1]
        column_ref[slot, 0] = dot(real, hot).astype(jnp.bfloat16)
        column_ref[slot, 1] = dot(imag, hot).astype(jnp.bfloat16)
        slope_real = dot(table, real).astype(jnp.bfloat16)
        slope_imag = dot(table, imag).astype(jnp.bfloat16)
        near_real, near_imag = parts_of(green_r[slot])
        plain = dot(near_real, real) - dot(near_imag, imag)
        slope_x = dot(near_imag, slope_real[:cells]) + dot(near_real, slope_imag[:cells])
        slope_y = dot(near_imag, slope_real[cells:]) + dot(near_real, slope_imag[cells:])
        sound = sound + plain * (weight * weight * profile_ref[0] * scale)
        along_x = along_x + slope_x * (weight * scale)
        along_y = along_y + slope_y * (weight * scale)
    for k, products in enumerate([sound, along_x, along_y]):
        out_ref[k] = pick_receivers(pick_sources(products, hot), receiver_ref)


def parts_of(rows):
    parts = jnp.swapaxes(rows, 0, 1)
    return parts[0], parts[1]


def layer_term(weight_ref, receiver_ref, column_ref, other_r, first=0):
    total = 0.0
    for slot in range(first, first + other_r.shape[0]):
        real, imag = parts_of(other_r[slot - first])
        both = dot(imag, column_ref[slot, 0]) + dot(real, column_ref[slot, 1])
        total = total + both * weight_ref[slot]
    return pick_receivers(total, receiver_ref)


def half_term(weight_ref, receiver_ref, column_ref, near_r, out_ref):
    out_ref[...] = layer_term(weight_ref, receiver_ref, column_ref, near_r)


def moved(value, share, to, part):
    return pltpu.roll(value, (to - part) * share % LANES, 1) if to != part else value


def base_rows(share, weight_ref, receiver_ref, column_ref, near_r, terms, out_ref):
    near = layer_term(weight_ref, receiver_ref, column_ref, near_r)
    odd = lax.rem(lax.axis_index("depth"), 2) == 1
    below = jnp.where(odd, 0.0, near)
    above = jnp.where(odd, near, 0.0)
    tiles = near.shape[0]
    group = lax.broadcasted_iota(jnp.int32, (tiles, LANES), 1) // share
    in_tile = LANES // share
    for part in range(in_tile):
        first = moved(below, share, 3, part)
        for k in range(3):
            first = jnp.where(group == k, moved(terms[k], share, k, part), first)
        out_ref[part] = first
        out_ref[in_tile + part] = moved(above, share, 0, part)


def far_term(share, weight_ref, receiver_ref, column_ref, far_r, base, half_ref, out_ref):
    first = column_ref.shape[0] - far_r.shape[0]
    far = half_ref[...] + layer_term(weight_ref, receiver_ref, column_ref, far_r, first)
    odd = lax.rem(lax.axis_index("depth"), 2) == 1
    below = jnp.where(odd, far, 0.0)
    above = jnp.where(odd, 0.0, far)
    tiles = far.shape[0]
    last = lax.broadcasted_iota(jnp.int32, (tiles, LANES), 1) // share == 3
    in_tile = LANES // share
    for part in range(in_tile):
        own = jnp.where(last, moved(below, share, 3, part), 0.0)
        out_ref[pl.ds(2 * part, tiles, stride=2 * in_tile), :] = base[part] + own
        out_ref[pl.ds(2 * part + 1, tiles, stride=2 * in_tile), :] = base[
            in_tile + part
        ] + moved(above, share, 0, part)


def combine(freqs, depths, share, parts_ref, out_ref):
    def row(which):
        total = parts_ref[pl.ds(which, depths, stride=2), :]
        for group in range(1, freqs):
            total = total + parts_ref[pl.ds(2 * group * depths + which, depths, stride=2), :]
        return total

    first, second = row(0), row(1)
    depth = lax.broadcasted_iota(jnp.int32, first.shape, 0)
    above = jnp.where(depth == depths - 1, 0.0, pltpu.roll(first, depths - 1, 0))
    below = jnp.where(depth == 0, 0.0, pltpu.roll(second, 1, 0))
    for k in range(3):
        out_ref[k] = pltpu.roll(first, (LANES - k * share) % LANES, 1)[:, :share]
    out_ref[3] = (pltpu.roll(above, LANES - 3 * share, 1) - below)[:, :share]


def vmem(count):
    return [pl.BlockSpec(memory_space=pltpu.VMEM)] * count


def smem(count):
    return [pl.BlockSpec(memory_space=pltpu.SMEM)] * count


def on_device(
    green_source, green_receiver, source_index, receiver_index, frequency_bins, depth_profile
):
    local_freqs, _, sources, _, cells = green_source.shape
    receivers = green_receiver.shape[2]
    pairs = source_index.shape[0]
    n_freq, n_depth = lax.axis_size("freq"), lax.axis_size("depth")
    owners = n_freq * n_depth
    share = pairs // owners
    tiles = pairs // LANES
    scale = 1.0 / math.sqrt(2.0 * WX * WY * local_freqs * n_freq)
    params = pltpu.CompilerParams(vmem_limit_bytes=VMEM_BYTES)

    own = green_receiver[:, 0]
    paired = [(i, i ^ 1) for i in range(n_depth)]
    crossed = [(i, i + 1) for i in range(1, n_depth - 1, 2)]
    crossed += [(target, source) for source, target in crossed]
    everywhere = [
        (group * n_depth + source, group * n_depth + target)
        for group in range(n_freq)
        for source, target in crossed
    ]
    everywhere += [
        (group * n_depth + end, (group ^ 1) * n_depth + end)
        for group in range(n_freq)
        for end in (0, n_depth - 1)
    ]
    half = local_freqs // 2
    far_r = lax.ppermute(own, ("freq", "depth"), everywhere)
    near_a = lax.ppermute(own[:half], "depth", paired)
    near_b = lax.ppermute(own[half:], "depth", paired)

    green_s = jnp.transpose(green_source[:, 0], (0, 2, 3, 1))
    source_row = source_index.reshape(1, pairs)
    receiver_row = receiver_index.reshape(1, pairs)
    product = 2 * 2 * cells * local_freqs * sources * receivers
    picking = 2 * 2 * sources * receivers * pairs

    def call(body, name, shapes, n_smem, n_vmem, terms):
        return pl.pallas_call(
            body,
            out_shape=shapes,
            in_specs=smem(n_smem) + vmem(n_vmem),
            out_specs=jax.tree.map(lambda _: pl.BlockSpec(memory_space=pltpu.VMEM), shapes),
            compiler_params=params,
            cost_estimate=pl.CostEstimate(
                flops=int(terms * (product + picking)), bytes_accessed=1 << 21, transcendentals=0
            ),
            name=name,
        )

    term_shape = jax.ShapeDtypeStruct((tiles, LANES), jnp.float32)
    terms, columns, weights = call(
        functools.partial(local_terms, scale),
        "local_terms",
        [
            jax.ShapeDtypeStruct((3, tiles, LANES), jnp.float32),
            jax.ShapeDtypeStruct((local_freqs, 2, cells, pairs), jnp.bfloat16),
            jax.ShapeDtypeStruct((local_freqs, 1, pairs), jnp.float32),
        ],
        2, 4, 3,
    )(frequency_bins, depth_profile, source_row, receiver_row, green_s, own)
    base = call(
        functools.partial(base_rows, share),
        "base_rows",
        jax.ShapeDtypeStruct((2 * LANES // share, tiles, LANES), jnp.float32),
        0, 5, 1,
    )(weights, receiver_row, columns, far_r, terms)
    halved = call(half_term, "half_term", term_shape, 0, 4, 0.5)(
        weights, receiver_row, columns, near_a
    )
    parts = call(
        functools.partial(far_term, share),
        "far_term",
        jax.ShapeDtypeStruct((2 * owners, LANES), jnp.float32),
        0, 6, 1,
    )(weights, receiver_row, columns, near_b, base, halved)
    parts = lax.all_to_all(parts, ("freq", "depth"), split_axis=0, concat_axis=0, tiled=True)
    kernels = call(
        functools.partial(combine, n_freq, n_depth, share),
        "combine",
        jax.ShapeDtypeStruct((4, n_depth, share), jnp.float32),
        0, 1, 0,
    )(parts)
    return jnp.swapaxes(kernels, 1, 2)


def solution(mesh):
    placed = (
        P("freq", "depth", None, None, None),
        P("freq", "depth", None, None, None),
        P(),
        P(),
        P("freq"),
        P("depth"),
    )
    return jax.shard_map(
        on_device,
        mesh=mesh,
        in_specs=placed,
        out_specs=P(None, ("freq", "depth"), None),
        check_vma=False,
    )
```

```python
import functools
import math

import jax
import jax.numpy as jnp
from jax import lax
from jax.experimental import pallas as pl
from jax.experimental.pallas import tpu as pltpu
from jax.sharding import PartitionSpec as P

NBINS = 128
WX = 16
WY = 16
LANES = 128
VMEM_BYTES = 48 * 1024 * 1024


def dot(left, right):
    return jnp.dot(left, right, preferred_element_type=jnp.float32)


def frequency_weight(bins_ref, slot):
    return 0.5 + bins_ref[slot].astype(jnp.float32) / NBINS


def slope_table(cells):
    target = lax.broadcasted_iota(jnp.int32, (cells, cells), 0)
    source = lax.broadcasted_iota(jnp.int32, (cells, cells), 1)
    column = lax.rem(target, WY)
    step = source - target
    half, zero = jnp.float32(0.5), jnp.float32(0.0)
    along_x = jnp.where(step == WY, half, zero) - jnp.where(step == -WY, half, zero)
    along_y = jnp.where((step == 1) & (column != WY - 1), half, zero) - jnp.where(
        (step == -1) & (column != 0), half, zero
    )
    return jnp.concatenate([along_x, along_y], axis=0).astype(jnp.bfloat16)


def pick_sources(products, hot):
    receivers = products.shape[0]
    high = products.astype(jnp.bfloat16)
    low = (products - high.astype(jnp.float32)).astype(jnp.bfloat16)
    both = dot(jnp.concatenate([high, low], axis=0), hot)
    return both[:receivers] + both[receivers:]


def pick_receivers(picked, receiver_ref):
    receivers, pairs = picked.shape
    at_receiver = lax.broadcasted_iota(jnp.int32, (receivers, pairs), 0) == receiver_ref[...]
    row = jnp.sum(jnp.where(at_receiver, picked, 0.0), axis=0, keepdims=True)
    return jnp.concatenate(
        [row[:, at : at + LANES] for at in range(0, pairs, LANES)], axis=0
    )


def local_terms(
    scale,
    bins_ref,
    profile_ref,
    source_ref,
    receiver_ref,
    green_s,
    green_r,
    out_ref,
    column_ref,
    weight_ref,
):
    freqs, _, cells, sources = green_s.shape
    pairs = source_ref.shape[1]
    at_source = lax.broadcasted_iota(jnp.int32, (sources, pairs), 0) == source_ref[...]
    hot = jnp.where(at_source, jnp.float32(1), jnp.float32(0)).astype(jnp.bfloat16)
    table = slope_table(cells)
    sound = along_x = along_y = 0.0
    for slot in range(freqs):
        weight = frequency_weight(bins_ref, slot)
        weight_ref[slot] = jnp.full(weight_ref.shape[1:], 0.5 * weight * scale, jnp.float32)
        real, imag = green_s[slot, 0], green_s[slot, 1]
        column_ref[slot, 0] = dot(real, hot).astype(jnp.bfloat16)
        column_ref[slot, 1] = dot(imag, hot).astype(jnp.bfloat16)
        slope_real = dot(table, real).astype(jnp.bfloat16)
        slope_imag = dot(table, imag).astype(jnp.bfloat16)
        near_real, near_imag = parts_of(green_r[slot])
        plain = dot(near_real, real) - dot(near_imag, imag)
        slope_x = dot(near_imag, slope_real[:cells]) + dot(near_real, slope_imag[:cells])
        slope_y = dot(near_imag, slope_real[cells:]) + dot(near_real, slope_imag[cells:])
        sound = sound + plain * (weight * weight * profile_ref[0] * scale)
        along_x = along_x + slope_x * (weight * scale)
        along_y = along_y + slope_y * (weight * scale)
    for k, products in enumerate([sound, along_x, along_y]):
        out_ref[k] = pick_receivers(pick_sources(products, hot), receiver_ref)


def parts_of(rows):
    parts = jnp.swapaxes(rows, 0, 1)
    return parts[0], parts[1]


def layer_term(weight_ref, receiver_ref, column_ref, other_r, first=0):
    total = 0.0
    for slot in range(first, first + other_r.shape[0]):
        real, imag = parts_of(other_r[slot - first])
        both = dot(imag, column_ref[slot, 0]) + dot(real, column_ref[slot, 1])
        total = total + both * weight_ref[slot]
    return pick_receivers(total, receiver_ref)


def half_term(weight_ref, receiver_ref, column_ref, near_r, out_ref):
    out_ref[...] = layer_term(weight_ref, receiver_ref, column_ref, near_r)


def moved(value, share, to, part):
    return pltpu.roll(value, (to - part) * share % LANES, 1) if to != part else value


def base_rows(share, weight_ref, receiver_ref, column_ref, near_r, terms, out_ref):
    near = layer_term(weight_ref, receiver_ref, column_ref, near_r)
    odd = lax.rem(lax.axis_index("depth"), 2) == 1
    below = jnp.where(odd, 0.0, near)
    above = jnp.where(odd, near, 0.0)
    tiles = near.shape[0]
    group = lax.broadcasted_iota(jnp.int32, (tiles, LANES), 1) // share
    in_tile = LANES // share
    for part in range(in_tile):
        first = moved(below, share, 3, part)
        for k in range(3):
            first = jnp.where(group == k, moved(terms[k], share, k, part), first)
        out_ref[part] = first
        out_ref[in_tile + part] = moved(above, share, 3, part)


def far_term(share, weight_ref, receiver_ref, column_ref, far_r, base, half_ref, out_ref):
    first = column_ref.shape[0] - far_r.shape[0]
    far = half_ref[...] + layer_term(weight_ref, receiver_ref, column_ref, far_r, first)
    odd = lax.rem(lax.axis_index("depth"), 2) == 1
    below = jnp.where(odd, far, 0.0)
    above = jnp.where(odd, 0.0, far)
    tiles = far.shape[0]
    last = lax.broadcasted_iota(jnp.int32, (tiles, LANES), 1) // share == 3
    in_tile = LANES // share
    for part in range(in_tile):
        own = jnp.where(last, moved(below, share, 3, part), 0.0)
        out_ref[pl.ds(2 * part, tiles, stride=2 * in_tile), :] = base[part] + own
        out_ref[pl.ds(2 * part + 1, tiles, stride=2 * in_tile), :] = base[
            in_tile + part
        ] + moved(above, share, 3, part)


def combine(freqs, depths, share, parts_ref, out_ref):
    def row(which):
        total = parts_ref[pl.ds(which, depths, stride=2), :]
        for group in range(1, freqs):
            total = total + parts_ref[pl.ds(2 * group * depths + which, depths, stride=2), :]
        return total

    first, second = row(0), row(1)
    depth = lax.broadcasted_iota(jnp.int32, first.shape, 0)
    above = jnp.where(depth == depths - 1, 0.0, pltpu.roll(first, depths - 1, 0))
    below = jnp.where(depth == 0, 0.0, pltpu.roll(second, 1, 0))
    for k in range(3):
        out_ref[k] = pltpu.roll(first, (LANES - k * share) % LANES, 1)[:, :share]
    out_ref[3] = pltpu.roll(above - below, LANES - 3 * share, 1)[:, :share]


def vmem(count):
    return [pl.BlockSpec(memory_space=pltpu.VMEM)] * count


def smem(count):
    return [pl.BlockSpec(memory_space=pltpu.SMEM)] * count


def on_device(
    green_source, green_receiver, source_index, receiver_index, frequency_bins, depth_profile
):
    local_freqs, _, sources, _, cells = green_source.shape
    receivers = green_receiver.shape[2]
    pairs = source_index.shape[0]
    n_freq, n_depth = lax.axis_size("freq"), lax.axis_size("depth")
    owners = n_freq * n_depth
    share = pairs // owners
    tiles = pairs // LANES
    scale = 1.0 / math.sqrt(2.0 * WX * WY * local_freqs * n_freq)
    params = pltpu.CompilerParams(vmem_limit_bytes=VMEM_BYTES)

    own = green_receiver[:, 0]
    paired = [(i, i ^ 1) for i in range(n_depth)]
    crossed = [(i, i + 1) for i in range(1, n_depth - 1, 2)]
    crossed += [(target, source) for source, target in crossed]
    everywhere = [
        (group * n_depth + source, group * n_depth + target)
        for group in range(n_freq)
        for source, target in crossed
    ]
    everywhere += [
        (group * n_depth + end, (group ^ 1) * n_depth + end)
        for group in range(n_freq)
        for end in (0, n_depth - 1)
    ]
    half = local_freqs // 2
    far_r = lax.ppermute(own, ("freq", "depth"), everywhere)
    near_a = lax.ppermute(own[:half], "depth", paired)
    near_b = lax.ppermute(own[half:], "depth", paired)

    green_s = jnp.transpose(green_source[:, 0], (0, 2, 3, 1))
    source_row = source_index.reshape(1, pairs)
    receiver_row = receiver_index.reshape(1, pairs)
    product = 2 * 2 * cells * local_freqs * sources * receivers
    picking = 2 * 2 * sources * receivers * pairs

    def call(body, name, shapes, n_smem, n_vmem, terms):
        return pl.pallas_call(
            body,
            out_shape=shapes,
            in_specs=smem(n_smem) + vmem(n_vmem),
            out_specs=jax.tree.map(lambda _: pl.BlockSpec(memory_space=pltpu.VMEM), shapes),
            compiler_params=params,
            cost_estimate=pl.CostEstimate(
                flops=int(terms * (product + picking)), bytes_accessed=1 << 21, transcendentals=0
            ),
            name=name,
        )

    term_shape = jax.ShapeDtypeStruct((tiles, LANES), jnp.float32)
    terms, columns, weights = call(
        functools.partial(local_terms, scale),
        "local_terms",
        [
            jax.ShapeDtypeStruct((3, tiles, LANES), jnp.float32),
            jax.ShapeDtypeStruct((local_freqs, 2, cells, pairs), jnp.bfloat16),
            jax.ShapeDtypeStruct((local_freqs, 1, pairs), jnp.float32),
        ],
        2, 4, 3,
    )(frequency_bins, depth_profile, source_row, receiver_row, green_s, own)
    base = call(
        functools.partial(base_rows, share),
        "base_rows",
        jax.ShapeDtypeStruct((2 * LANES // share, tiles, LANES), jnp.float32),
        0, 5, 1,
    )(weights, receiver_row, columns, far_r, terms)
    halved = call(half_term, "half_term", term_shape, 0, 4, 0.5)(
        weights, receiver_row, columns, near_a
    )
    parts = call(
        functools.partial(far_term, share),
        "far_term",
        jax.ShapeDtypeStruct((2 * owners, LANES), jnp.float32),
        0, 6, 1,
    )(weights, receiver_row, columns, near_b, base, halved)
    parts = lax.all_to_all(parts, ("freq", "depth"), split_axis=0, concat_axis=0, tiled=True)
    kernels = call(
        functools.partial(combine, n_freq, n_depth, share),
        "combine",
        jax.ShapeDtypeStruct((4, n_depth, share), jnp.float32),
        0, 1, 0,
    )(parts)
    return jnp.swapaxes(kernels, 1, 2)


def solution(mesh):
    placed = (
        P("freq", "depth", None, None, None),
        P("freq", "depth", None, None, None),
        P(),
        P(),
        P("freq"),
        P("depth"),
    )
    return jax.shard_map(
        on_device,
        mesh=mesh,
        in_specs=placed,
        out_specs=P(None, ("freq", "depth"), None),
        check_vma=False,
    )
```
